256 devices in a mesh: lon: 16 (over z, core), lat: 16 (over x, y).
Axes of the slice: x: 4, y: 4, z: 8, core: 2. Of those that a mesh axis runs over, the one named last changes fastest.
Arguments:
- innovation: float32 [16384], P(('lon', 'lat')), may hold values from -6 to 6
- ray_id: int32 [16, 16, 64], P('lon', 'lat'), may hold values from 0 to 16383
- cell_index: int32 [16, 16, 64, 128], P('lon', 'lat'), may hold values from 0 to 131071
- seg_length: float32 [16, 16, 64, 128], P('lon', 'lat'), may hold values from 0.2 to 2
- vertical_modes: float32 [128, 128], replicated, may hold values from -2 to 2
- lon_decay: float32 [128, 512], replicated, as said below
- lat_decay: float32 [128, 512], replicated, as said below
Outputs:
- increment: float32 [512, 512, 128], P('lon', 'lat')
The draws below stay inside these ranges and needn't reach their ends.
Inputs may be any that keep to these rules, and one draw needn't show every extreme that they name: ray_id holds global observation indices. cell_index holds tile-local cell indices. `lon_decay`: every entry lies strictly between 0 and 1. `lat_decay`: every entry lies strictly between 0 and 1.
All inputs are finite; a program needn't handle non-finite values.
Results may differ from the reference program's by a relative error of at most 0.00018.
Values sent between devices are 32-bit elements; how exact they have to be, the bound alone decides.
A program may use at most 64 MiB of HBM per device.

```python
import math
import jax
import jax.numpy as jnp
from jax import lax

L = 128
M = 128
CL = 32
CT = 32
BLK_DEV = 64
SAMP = 128
NX = 512
NY = 512
RAYS = 16384
N_LON = 16
N_LAT = 16


def decay_table_draw(key, modes, cells, block, slow_share):
    keys = jax.random.split(key, 6)
    slow = jax.random.uniform(keys[0], (modes, 1)) < slow_share
    slow_rate = jax.random.uniform(keys[1], (modes, 1), minval=0.2, maxval=1.2) / cells
    fast_rate = 1.0 / (jax.random.uniform(keys[2], (modes, 1), minval=0.8, maxval=1.5) * block)
    base_rate = jnp.where(slow, slow_rate, fast_rate)
    rough = jnp.exp(jax.random.uniform(keys[3], (modes, cells), minval=jnp.log(0.6), maxval=jnp.log(1.6)))
    table = jnp.exp(-base_rate * rough)
    spots = jax.random.randint(keys[4], (3,), 0, cells)
    struck = jnp.any(jnp.arange(cells)[:, None] == spots[None, :], axis=1)
    depth = jax.random.uniform(keys[5], (modes, cells), minval=0.5, maxval=0.8)
    table = jnp.where(struck[None, :], table * depth, table)
    return table.astype(jnp.float32)


def draw_lon_decay(key, part):
    key = jax.random.fold_in(key, 11)
    share = 0.5
    return decay_table_draw(key, M, NX, CL, share)


def draw_lat_decay(key, part):
    key = jax.random.fold_in(key, 12)
    share = 0.5
    return decay_table_draw(key, M, NY, CT, share)


def set_ends(values, stream_key, least, high):
    index_at = [jax.random.randint(jax.random.fold_in(stream_key, axis), (), 0, length) for axis, length in enumerate(values.shape)]
    main_axis = values.shape.index(max(values.shape))
    neighbour = index_at[:main_axis] + [(index_at[main_axis] + 1) % values.shape[main_axis]] + index_at[main_axis + 1:]
    return values.at[tuple(index_at)].set(least).at[tuple(neighbour)].set(high)


def block_scale(key, extent, cuts, least, high):
    def one(dim, blocks):
        steps = jax.random.uniform(jax.random.fold_in(jax.random.fold_in(key, 6), dim), (blocks,), jnp.float32, least / len(cuts), high / len(cuts))
        return jnp.repeat(jnp.exp(steps), extent[dim] // blocks).reshape((-1,) + (1,) * (len(extent) - dim - 1))

    gain = one(*cuts[0])
    for cut in cuts[1:]:
        gain = gain * one(*cut)
    return gain


def gaussian(own_key, extent, spread, bound, cuts=(), held_as=jnp.bfloat16):
    drawn = jax.random.normal(own_key, extent, jnp.float32) * spread
    if len(cuts) > 0:
        drawn = block_scale(own_key, extent, cuts, -0.22, 0.18) * drawn
    return jnp.clip(drawn, min=-bound, max=bound).astype(held_as)


def setup_inputs(seed: int = 0) -> dict:
    seeds = jax.random.split(jax.random.key(seed), 8)
    return {
        "innovation": gaussian(seeds[0], (RAYS,), 1.0, 6.0, ((0, 256),), jnp.float32),
        "ray_id": set_ends(jax.random.randint(seeds[1], (N_LON, N_LAT, BLK_DEV), 0, RAYS), jax.random.fold_in(seeds[1], 1), 0, RAYS - 1).astype(jnp.int32),
        "cell_index": set_ends(jax.random.randint(seeds[2], (N_LON, N_LAT, BLK_DEV, SAMP), 0, CL * CT * L), jax.random.fold_in(seeds[2], 1), 0, (CL * CT * L) - 1).astype(jnp.int32),
        "seg_length": jnp.clip(jnp.exp(math.log(2.0) - 2.3025851 * jax.random.uniform(seeds[3], (N_LON, N_LAT, BLK_DEV, SAMP), jnp.float32) ** block_scale(seeds[3], (N_LON, N_LAT, BLK_DEV, SAMP), ((0, 16), (1, 16)), -0.2, 0.2)), 0.2, 2.0),
        "vertical_modes": gaussian(seeds[4], (L, M), (M // 16) ** -0.5, 2.0, (), jnp.float32),
        "lon_decay": draw_lon_decay(jax.random.fold_in(seeds[7], 71), 0),
        "lat_decay": draw_lat_decay(jax.random.fold_in(seeds[7], 71), 0),
    }


def recurse(coefficients, inputs, periodic):
    def advance(carried, element):
        carried = element[0][None, :] * carried + element[1]
        return carried, carried

    initial = jnp.zeros(inputs.shape[1:], jnp.float32)
    final_state, states = lax.scan(advance, initial, (coefficients, inputs))
    if periodic:
        growth = jnp.exp(jnp.cumsum(jnp.log(coefficients), 0))
        start_state = final_state / (1.0 - growth[-1])[None, :]
        states = states + growth[:, None, :] * start_state[None]
    return states


def smooth(grid_field, decay_table, periodic):
    coefficients = decay_table.T
    amplitude = (1.0 - coefficients) ** 0.75
    return recurse(coefficients, amplitude[:, None, :] * grid_field, periodic)


def smooth_adjoint(grid_field, decay_table, periodic):
    coefficients = jnp.roll(decay_table.T, -1, 0)
    amplitude = (1.0 - decay_table.T) ** 0.75
    states = recurse(coefficients[::-1], grid_field[::-1], periodic)[::-1]
    return amplitude[:, None, :] * states


def reference(innovation, ray_id, cell_index, seg_length, vertical_modes, lon_decay, lat_decay):
    tiles_lon = ray_id.shape[0]
    tiles_lat = ray_id.shape[1]
    values = seg_length * innovation[ray_id][..., None]
    column_of = cell_index // (CT * L)
    row_of = (cell_index // L) % CT
    level_of = cell_index % L
    lon_place = jnp.arange(tiles_lon, dtype=jnp.int32)[:, None, None, None] * CL + column_of
    lat_place = jnp.arange(tiles_lat, dtype=jnp.int32)[None, :, None, None] * CT + row_of
    flat_index = ((lon_place * NY + lat_place) * L + level_of).astype(jnp.int32)
    forcing = jax.ops.segment_sum(values.reshape(-1), flat_index.reshape(-1), num_segments=NX * NY * L)
    spectral = jnp.dot(forcing.reshape(NX * NY, L), vertical_modes, precision=lax.Precision.HIGHEST).reshape(NX, NY, M)
    spectral = smooth_adjoint(spectral, lon_decay, True)
    turned = jnp.swapaxes(spectral, 0, 1)
    turned = smooth(smooth_adjoint(turned, lat_decay, False), lat_decay, False)
    spectral = smooth(jnp.swapaxes(turned, 0, 1), lon_decay, True)
    result = jnp.dot(spectral.reshape(NX * NY, M), vertical_modes.T, precision=lax.Precision.HIGHEST)
    return result.reshape(NX, NY, L)
```

```python
import functools

import jax
import jax.numpy as jnp
from jax import lax
from jax.experimental import pallas as pl
from jax.experimental.pallas import tpu as pltpu
from jax.sharding import PartitionSpec as P

MESH = pl.DeviceIdType.MESH
BF = jnp.bfloat16
F32 = jnp.float32
CELLS = 32
TILES = 16
MODES = 128
ROWS = CELLS * CELLS
BLOCKS = 64
SAMP = 128
LAT_PEERS = (10, 2, 8, 9, 11, 6, 14, 5, 7, 13, 15, 1, 3, 4, 12)
LON_PEERS = (8, 9, 7, 6, 10, 5, 11, 4, 12, 3, 13, 2, 14, 1, 15)
CHIP_PEERS = (4, 3, 5, 2, 6, 1, 7)


def split(value):
    high = value.astype(BF)
    return high, (value - high.astype(F32)).astype(BF)


def one_hot_rows(cell_ref, cells_hot, start, stop):
    def body(block, _):
        cell = cell_ref[pl.ds(block, 1), :]
        lon = lax.shift_right_logical(cell, 12)
        lat = jnp.bitwise_and(lax.shift_right_logical(cell, 7), CELLS - 1)
        place = lax.broadcasted_iota(jnp.int32, (CELLS, SAMP), 0)
        lat_hot = (place == lat).astype(F32).astype(BF)
        lon_hot = (place == lon).astype(F32)
        for row in range(CELLS):
            chosen = jnp.broadcast_to(lon_hot[row : row + 1], (CELLS, SAMP)).astype(BF)
            cells_hot[block, row * CELLS : (row + 1) * CELLS] = lat_hot * chosen
        return 0

    lax.fori_loop(start, stop, body, 0)


def valued_levels(cell_ref, value_ref, block):
    level = jnp.bitwise_and(cell_ref[pl.ds(block, 1), :], MODES - 1)
    hit = lax.broadcasted_iota(jnp.int32, (MODES, SAMP), 0) == level
    value = value_ref[pl.ds(block, 1), :]
    high = value.astype(BF).astype(F32)
    low = value - high
    return jnp.concatenate(
        [jnp.where(hit, high, 0.0).astype(BF), jnp.where(hit, low, 0.0).astype(BF)], axis=0
    )


def scatter(cell_ref, value_ref, cells_hot, acc, step=16):
    acc[...] = jnp.zeros_like(acc)

    def body(chunk, _):
        total = None
        for inner in range(0, step, 2):
            block = chunk * step + inner
            levels = jnp.concatenate(
                [valued_levels(cell_ref, value_ref, block + k) for k in range(2)], axis=1
            )
            cells = jnp.concatenate([cells_hot[block], cells_hot[block + 1]], axis=1)
            part = lax.dot_general(
                cells, levels, (((1,), (1,)), ((), ())), preferred_element_type=F32
            )
            total = part if total is None else total + part
        acc[...] += total
        return 0

    lax.fori_loop(0, BLOCKS // step, body, 0)


def tile_sums(table):
    def body(cell, carried):
        grow, var, gap = carried
        decay = table[pl.ds(cell, TILES, stride=CELLS), :]
        less = 1.0 - decay
        return (
            grow * decay,
            decay * decay * var + less * jnp.sqrt(less),
            gap + grow * less,
        )

    zero = jnp.zeros((TILES, MODES), F32)
    return lax.fori_loop(0, CELLS, body, (zero + 1.0, zero, zero))


def own_tables(table, first, var, decay_ref, var_ref, enter_ref, leave_ref):
    decay_ref[...] = table[pl.ds(pl.multiple_of(first, CELLS), CELLS), :]
    grow = jnp.ones((1, MODES), F32)
    for cell in range(CELLS):
        decay = decay_ref[cell : cell + 1, :]
        less = 1.0 - decay
        var = decay * decay * var + less * jnp.sqrt(less)
        grow = grow * decay
        var_ref[cell : cell + 1, :] = var
        enter_ref[cell : cell + 1, :] = grow
    grow = jnp.ones((1, MODES), F32)
    for cell in reversed(range(CELLS)):
        leave_ref[cell : cell + 1, :] = grow * var_ref[cell : cell + 1, :]
        grow = grow * decay_ref[cell : cell + 1, :]


def kernel(
    innov_hbm, ray_hbm, cell_hbm, seg_hbm, modes_hbm, lon_hbm, lat_hbm, out_ref,
    innov_ref, ray_ref, cell_ref, seg_ref, modes_ref, lon_ref, lat_ref, in_sems,
    cells_hot, acc, field, value, innov_row, all_innov, g1_buf,
    lon_table, lat_table, lon_grow, lat_grow, chip_grow,
    lon_decay, lon_var, lon_enter, lon_leave, lat_decay, lat_var, lat_enter, lat_leave,
    lon_state, pair_buf, chip_buf, lon_carry, lat_state, lat_buf, lon_corner, lat_corner,
    smooth, lon_total, lat_total,
    g1_send, g1_recv, g2_send, g2_recv, t1_send, t1_recv, t2_send, t2_recv,
    b1_send, b1_recv, l2_send, l2_recv, pair_send, pair_recv,
):
    loads = [
        pltpu.make_async_copy(src, dst, in_sems.at[k])
        for k, (src, dst) in enumerate(
            (
                (innov_hbm, innov_ref),
                (lon_hbm, lon_ref),
                (lat_hbm, lat_ref),
                (cell_hbm, cell_ref),
                (ray_hbm, ray_ref),
                (seg_hbm, seg_ref),
                (modes_hbm, modes_ref),
            )
        )
    ]
    for load in loads:
        load.start()
    innov_in, lon_in, lat_in, *late_in = loads
    p, q = lax.axis_index("lon"), lax.axis_index("lat")
    z, core = p // 2, p % 2
    q_bits = [(q // 2**k) % 2 for k in range(4)]
    partner = p + 1 - 2 * core

    def lat_peer(mask):
        peer = q
        for k in range(4):
            if (mask >> k) & 1:
                peer = peer + (1 - 2 * q_bits[k]) * 2**k
        return peer

    def lat_slot(tile):
        slot = 0
        for k in range(4):
            bit = 1 - q_bits[k] if (tile >> k) & 1 else q_bits[k]
            slot = slot + bit * 2**k
        return slot

    def lon_peer(offset):
        return (p + offset) % TILES

    barrier = pltpu.get_barrier_semaphore()
    for offset in LON_PEERS:
        pl.semaphore_signal(
            barrier, inc=1, device_id={"lon": lon_peer(offset)}, device_id_type=MESH
        )
    for mask in LAT_PEERS:
        pl.semaphore_signal(
            barrier, inc=1, device_id={"lat": lat_peer(mask)}, device_id_type=MESH
        )

    sent = []

    def push(src, dst, send_sem, recv_sem, device):
        copy = pltpu.make_async_remote_copy(
            src_ref=src, dst_ref=dst, send_sem=send_sem, recv_sem=recv_sem,
            device_id=device, device_id_type=MESH,
        )
        copy.start()
        sent.append(copy)
        return copy

    innov_row[...] = jnp.zeros_like(innov_row)
    innov_in.wait()
    innov_row[0:1, 0:64] = innov_ref[...]
    row = jnp.broadcast_to(innov_row[0:1, :], (8, 128))
    both = row + pltpu.roll(row, 64, 1)
    sub = lax.broadcasted_iota(jnp.int32, (8, 128), 0)
    lane = lax.broadcasted_iota(jnp.int32, (8, 128), 1)
    mine = (sub == q // 2) & (lane // 64 == q % 2)
    g1_buf[0] = jnp.where(mine, both, 0.0)

    pl.semaphore_wait(barrier, 2 * (TILES - 1))
    g1 = [
        push(g1_buf.at[0], g1_buf.at[m], g1_send.at[m], g1_recv.at[m], {"lat": lat_peer(m)})
        for m in LAT_PEERS
    ]

    lon_in.wait()
    lat_in.wait()
    for part in range(4):
        span = slice(part * 128, (part + 1) * 128)
        lon_table[span, :] = lon_ref[:, span].T
        lat_table[span, :] = lat_ref[:, span].T
    grow, var, gap = tile_sums(lon_table)
    lon_grow[...] = grow
    loop, loop_gap, loop_var = grow[0:1], gap[0:1], var[0:1]
    for tile in range(1, TILES):
        own = slice(tile, tile + 1)
        loop_var = grow[own] * grow[own] * loop_var + var[own]
        loop_gap = loop_gap + loop * gap[own]
        loop = loop * grow[own]
    enter_var = loop_var / (loop_gap * (1.0 + loop))
    for tile in range(TILES - 1):
        own = slice(tile, tile + 1)
        enter_var = jnp.where(
            tile < p, grow[own] * grow[own] * enter_var + var[own], enter_var
        )
    own_tables(lon_table, p * CELLS, enter_var, lon_decay, lon_var, lon_enter, lon_leave)
    loop_scale = 1.0 / loop_gap
    for chip in range(TILES // 2):
        chip_grow[chip : chip + 1, :] = grow[2 * chip : 2 * chip + 1] * grow[2 * chip + 1 : 2 * chip + 2]

    grow, var, gap = tile_sums(lat_table)
    lat_grow[...] = grow
    enter_var = jnp.zeros((1, MODES), F32)
    for tile in range(TILES - 1):
        own = slice(tile, tile + 1)
        enter_var = jnp.where(
            tile < q, grow[own] * grow[own] * enter_var + var[own], enter_var
        )
    own_tables(lat_table, q * CELLS, enter_var, lat_decay, lat_var, lat_enter, lat_leave)

    for load in late_in:
        load.wait()
    one_hot_rows(cell_ref, cells_hot, 0, BLOCKS // 4)

    for copy in g1:
        copy.wait_recv()
    total = g1_buf[0]
    for slot in range(1, TILES):
        total = total + g1_buf[slot]
    all_innov[p] = total
    g2 = [
        push(all_innov.at[p], all_innov.at[p], g2_send.at[o], g2_recv.at[o], {"lon": lon_peer(o)})
        for o in LON_PEERS
    ]

    one_hot_rows(cell_ref, cells_hot, BLOCKS // 4, BLOCKS)
    ray = jnp.broadcast_to(ray_ref[...].astype(F32), (BLOCKS, BLOCKS))
    diagonal = lax.broadcasted_iota(jnp.int32, (BLOCKS, BLOCKS), 0) == lax.broadcasted_iota(
        jnp.int32, (BLOCKS, BLOCKS), 1
    )
    ray = jnp.sum(jnp.where(diagonal, ray, 0.0), axis=1, keepdims=True).astype(jnp.int32)
    ray = jnp.broadcast_to(ray, (BLOCKS, 128))
    place = lax.broadcasted_iota(jnp.int32, (BLOCKS, 128), 1)
    row_hot = (place == ray // 128).astype(F32).astype(BF)
    lane_hot = place == ray % 128

    for copy in g2:
        copy.wait_recv()
    table = all_innov[...].reshape(128, 128)
    picked = jnp.zeros((BLOCKS, 128), F32)
    for _ in range(3):
        high = table.astype(BF)
        picked = picked + jnp.dot(row_hot, high, preferred_element_type=F32)
        table = table - high.astype(F32)
    picked = jnp.sum(jnp.where(lane_hot, picked, 0.0), axis=1, keepdims=True)
    value[...] = seg_ref[...] * picked

    scatter(cell_ref, value, cells_hot, acc)

    modes_high, modes_low = split(modes_ref[...])
    both = jnp.concatenate([modes_high, modes_low], axis=1)
    to_modes = jnp.concatenate([both, both], axis=0)

    def to_spectral(chunk, _):
        own = pl.ds(pl.multiple_of(chunk * 256, 256), 256)
        forcing = acc[own, 0:128] + acc[own, 128:256]
        parts = jnp.concatenate(split(forcing), axis=1)
        result = jnp.dot(parts, to_modes, preferred_element_type=F32)
        field[own, :] = result[:, 0:128] + result[:, 128:256]
        return 0

    lax.fori_loop(0, ROWS // 256, to_spectral, 0)

    def lon_rows(cell):
        return pl.ds(cell * CELLS, CELLS) if isinstance(cell, int) else pl.ds(
            pl.multiple_of(cell * CELLS, CELLS), CELLS
        )

    state = jnp.zeros((CELLS, MODES), F32)
    for cell in range(CELLS):
        own = slice(cell, cell + 1)
        state = lon_decay[own] * state + lon_var[own] * field[lon_rows(cell), :]
        smooth[lon_rows(cell), :] = state
    lon_state[0] = state
    back = jnp.zeros((CELLS, MODES), F32)
    for cell in reversed(range(CELLS)):
        own = slice(cell, cell + 1)
        smooth[lon_rows(cell), :] = smooth[lon_rows(cell), :] + lon_var[own] * back
        back = lon_decay[own] * (back + field[lon_rows(cell), :])
    lon_state[1] = back

    def corners(state):
        return (
            jnp.sum(lat_leave[...] * state, axis=0, keepdims=True),
            jnp.sum(lat_enter[...] * state, axis=0, keepdims=True),
        )

    ff, fb = corners(lon_state[0])
    bf_, bb = corners(lon_state[1])
    lon_corner[0] = jnp.concatenate([ff, fb, bf_, bb, jnp.zeros((4, MODES), F32)], axis=0)
    t1 = [
        push(lon_corner.at[0], lon_corner.at[o], t1_send.at[o], t1_recv.at[o], {"lon": lon_peer(o)})
        for o in LON_PEERS
    ]
    l1 = push(lon_state.at[1 - core], pair_buf, pair_send.at[0], pair_recv.at[0], {"lon": partner})

    state = jnp.zeros((CELLS, MODES), F32)
    for cell in range(CELLS):
        own = slice(cell, cell + 1)
        rows = pl.ds(cell, CELLS, stride=CELLS)
        state = lat_decay[own] * state + lat_var[own] * smooth[rows, :]
        field[rows, :] = state
    lat_state[0] = state
    back = jnp.zeros((CELLS, MODES), F32)
    for cell in reversed(range(CELLS)):
        own = slice(cell, cell + 1)
        rows = pl.ds(cell, CELLS, stride=CELLS)
        field[rows, :] = field[rows, :] + lat_var[own] * back
        back = lat_decay[own] * (back + smooth[rows, :])
    lat_state[1] = back

    l1.wait_recv()
    chip_state = pair_buf[...] + lon_grow[pl.ds(partner, 1), :] * lon_state[core]
    chip_buf[0] = chip_state
    sign = 1 - 2 * core
    l2 = [
        push(
            chip_buf.at[0], chip_buf.at[o], l2_send.at[o], l2_recv.at[o],
            {"lon": 2 * ((z + sign * o + 8) % 8) + core},
        )
        for o in CHIP_PEERS
    ]
    b1 = []
    for m in LAT_PEERS:
        top = m.bit_length() - 1
        b1.append(
            push(
                lat_state.at[q_bits[top]], lat_buf.at[m], b1_send.at[m], b1_recv.at[m],
                {"lat": lat_peer(m)},
            )
        )
    lat_buf[0] = lat_state[0]

    for copy in t1:
        copy.wait_recv()
    ahead = lon_corner[0]
    behind = lon_corner[0]
    for o in reversed(range(1, TILES)):
        ahead = lon_grow[pl.ds((p + TILES - o) % TILES, 1), :] * ahead + lon_corner[o]
        behind = lon_grow[pl.ds((p + o) % TILES, 1), :] * behind + lon_corner[TILES - o]
    sub = lax.broadcasted_iota(jnp.int32, (8, MODES), 0)
    lat_corner[0] = jnp.where(sub < 2, ahead, behind) * loop_scale
    t2 = [
        push(lat_corner.at[0], lat_corner.at[m], t2_send.at[m], t2_recv.at[m], {"lat": lat_peer(m)})
        for m in LAT_PEERS
    ]

    for copy in l2:
        copy.wait_recv()
    carry = chip_buf[0]
    for o in reversed(range(1, 8)):
        carry = chip_grow[pl.ds((z - sign * o + 8) % 8, 1), :] * carry + chip_buf[o]
    carry = carry * loop_scale
    lon_carry[core] = carry
    pair_buf[...] = lon_grow[pl.ds(p, 1), :] * carry + lon_state[core]
    l3 = push(pair_buf, lon_carry.at[core], pair_send.at[1], pair_recv.at[1], {"lon": partner})

    for copy in b1:
        copy.wait_recv()
    ahead = jnp.zeros((CELLS, MODES), F32)
    behind = jnp.zeros((CELLS, MODES), F32)
    for tile in range(TILES - 1):
        got = lat_buf[lat_slot(tile)]
        ahead = jnp.where(tile < q, lat_grow[tile : tile + 1, :] * ahead + got, ahead)
    for tile in reversed(range(1, TILES)):
        got = lat_buf[lat_slot(tile)]
        behind = jnp.where(tile > q, lat_grow[tile : tile + 1, :] * behind + got, behind)

    l3.wait_recv()
    for way in range(2):
        state = jnp.zeros((1, MODES), F32)
        back = jnp.zeros((1, MODES), F32)
        for cell in range(CELLS):
            own = slice(cell, cell + 1)
            state = lat_decay[own] * state + lat_var[own] * lon_carry[way, own, :]
            lon_total[way, own, :] = state
        for cell in reversed(range(CELLS)):
            own = slice(cell, cell + 1)
            lon_total[way, own, :] = lon_total[way, own, :] + lat_var[own] * back
            back = lat_decay[own] * (back + lon_carry[way, own, :])

    for copy in t2:
        copy.wait_recv()
    corner_ahead = jnp.zeros((8, MODES), F32)
    corner_behind = jnp.zeros((8, MODES), F32)
    for tile in range(TILES - 1):
        got = lat_corner[lat_slot(tile)]
        corner_ahead = jnp.where(
            tile < q, lat_grow[tile : tile + 1, :] * corner_ahead + got, corner_ahead
        )
    for tile in reversed(range(1, TILES)):
        got = lat_corner[lat_slot(tile)]
        corner_behind = jnp.where(
            tile > q, lat_grow[tile : tile + 1, :] * corner_behind + got, corner_behind
        )
    lat_total[0] = ahead + lon_enter[...] * corner_ahead[0:1] + lon_leave[...] * corner_ahead[2:3]
    lat_total[1] = behind + lon_enter[...] * corner_behind[1:2] + lon_leave[...] * corner_behind[3:4]

    both = jnp.concatenate([modes_high, modes_low], axis=0)
    to_levels = jnp.concatenate([both, both], axis=1)
    per = 8

    def to_grid(chunk, _):
        pieces = []
        for inner in range(per):
            cell = chunk * per + inner
            own = pl.ds(cell, 1)
            pieces.append(
                field[lon_rows(cell), :]
                + lon_enter[own, :] * lon_total[0]
                + lon_leave[own, :] * lon_total[1]
                + lat_enter[...] * lat_total[0, own, :]
                + lat_leave[...] * lat_total[1, own, :]
            )
        whole = jnp.concatenate(pieces, axis=0)
        parts = jnp.concatenate(split(whole), axis=1)
        result = lax.dot_general(
            parts, to_levels, (((1,), (1,)), ((), ())), preferred_element_type=F32
        )
        own = pl.ds(pl.multiple_of(chunk * (per * CELLS), per * CELLS), per * CELLS)
        out_ref[own, :] = result[:, 0:128] + result[:, 128:256]
        return 0

    lax.fori_loop(0, CELLS // per, to_grid, 0)

    for copy in sent:
        copy.wait_send()


def on_device(innovation, ray_id, cell_index, seg_length, vertical_modes, lon_decay, lat_decay):
    vmem = pl.BlockSpec(memory_space=pltpu.VMEM)
    tile = lambda *shape: pltpu.VMEM(shape, F32)
    sems = lambda count: pltpu.SemaphoreType.DMA((count,))
    result = pl.pallas_call(
        kernel,
        out_shape=jax.ShapeDtypeStruct((ROWS, MODES), F32),
        in_specs=[pl.BlockSpec(memory_space=pltpu.HBM)] * 7,
        out_specs=vmem,
        scratch_shapes=[
            tile(1, 64),
            pltpu.VMEM((1, BLOCKS), jnp.int32),
            pltpu.VMEM((BLOCKS, SAMP), jnp.int32),
            tile(BLOCKS, SAMP),
            tile(MODES, MODES),
            tile(MODES, TILES * CELLS),
            tile(MODES, TILES * CELLS),
            pltpu.SemaphoreType.DMA((7,)),
            pltpu.VMEM((BLOCKS, ROWS, SAMP), BF),
            tile(ROWS, 256),
            tile(ROWS, MODES),
            tile(BLOCKS, SAMP),
            tile(8, 128),
            tile(TILES, 8, 128),
            tile(TILES, 8, 128),
            tile(TILES * CELLS, MODES),
            tile(TILES * CELLS, MODES),
            tile(TILES, MODES),
            tile(TILES, MODES),
            tile(TILES // 2, MODES),
        ]
        + [tile(CELLS, MODES)] * 8
        + [
            tile(2, CELLS, MODES),
            tile(CELLS, MODES),
            tile(8, CELLS, MODES),
            tile(2, CELLS, MODES),
            tile(2, CELLS, MODES),
            tile(TILES, CELLS, MODES),
            tile(TILES, 8, MODES),
            tile(TILES, 8, MODES),
            tile(ROWS, MODES),
            tile(2, CELLS, MODES),
            tile(2, CELLS, MODES),
        ]
        + [sems(TILES)] * 10
        + [sems(8)] * 2
        + [sems(2)] * 2,
        compiler_params=pltpu.CompilerParams(
            collective_id=0, has_side_effects=True, vmem_limit_bytes=63 * 2**20
        ),
        name="covariance",
    )(
        innovation.reshape(1, 64),
        ray_id.reshape(1, BLOCKS),
        cell_index.reshape(BLOCKS, SAMP),
        seg_length.reshape(BLOCKS, SAMP),
        vertical_modes,
        lon_decay,
        lat_decay,
    )
    return result.reshape(CELLS, CELLS, MODES)


def solution(mesh):
    placed = (
        P(("lon", "lat")),
        P("lon", "lat", None),
        P("lon", "lat", None, None),
        P("lon", "lat", None, None),
        P(),
        P(),
        P(),
    )
    return jax.shard_map(
        on_device, mesh=mesh, in_specs=placed, out_specs=P("lon", "lat", None), check_vma=False
    )
```

```python
import functools

import jax
import jax.numpy as jnp
from jax import lax
from jax.experimental import pallas as pl
from jax.experimental.pallas import tpu as pltpu
from jax.sharding import PartitionSpec as P

MESH = pl.DeviceIdType.MESH
BF = jnp.bfloat16
F32 = jnp.float32
CELLS = 32
TILES = 16
MODES = 128
ROWS = CELLS * CELLS
BLOCKS = 64
SAMP = 128
LAT_PEERS = (10, 2, 8, 9, 11, 6, 14, 5, 7, 13, 15, 1, 3, 4, 12)
LON_PEERS = (8, 9, 7, 6, 10, 5, 11, 4, 12, 3, 13, 2, 14, 1, 15)
CHIP_PEERS = (4, 3, 5, 2, 6, 1, 7)


def split(value):
    high = value.astype(BF)
    return high, (value - high.astype(F32)).astype(BF)


def one_hot_rows(cell_ref, cells_hot, start, stop):
    def body(block, _):
        cell = cell_ref[pl.ds(block, 1), :]
        lon = lax.shift_right_logical(cell, 12)
        lat = jnp.bitwise_and(lax.shift_right_logical(cell, 7), CELLS - 1)
        place = lax.broadcasted_iota(jnp.int32, (CELLS, SAMP), 0)
        lat_hot = (place == lat).astype(F32).astype(BF)
        lon_hot = (place == lon).astype(F32)
        for row in range(CELLS):
            chosen = jnp.broadcast_to(lon_hot[row : row + 1], (CELLS, SAMP)).astype(BF)
            cells_hot[block, row * CELLS : (row + 1) * CELLS] = lat_hot * chosen
        return 0

    lax.fori_loop(start, stop, body, 0)


def valued_levels(cell_ref, value_ref, block):
    level = jnp.bitwise_and(cell_ref[pl.ds(block, 1), :], MODES - 1)
    hit = lax.broadcasted_iota(jnp.int32, (MODES, SAMP), 0) == level
    value = value_ref[pl.ds(block, 1), :]
    high = value.astype(BF).astype(F32)
    low = value - high
    return jnp.concatenate(
        [jnp.where(hit, high, 0.0).astype(BF), jnp.where(hit, low, 0.0).astype(BF)], axis=0
    )


def scatter(cell_ref, value_ref, cells_hot, acc, start, stop, step=16):
    if start == 0:
        acc[...] = jnp.zeros_like(acc)

    def body(chunk, _):
        total = None
        for inner in range(0, step, 2):
            block = chunk * step + inner
            levels = jnp.concatenate(
                [valued_levels(cell_ref, value_ref, block + k) for k in range(2)], axis=1
            )
            cells = jnp.concatenate([cells_hot[block], cells_hot[block + 1]], axis=1)
            part = lax.dot_general(
                cells, levels, (((1,), (1,)), ((), ())), preferred_element_type=F32
            )
            total = part if total is None else total + part
        acc[...] += total
        return 0

    lax.fori_loop(start, stop, body, 0)


def early_sums(cell_ref, seg_ref, tables, early, start, stop, step=16):
    modes_table, lon_weights = tables
    width = step * SAMP

    def body(part, _):
        first = part * step

        def row(ref):
            return jnp.concatenate([ref[pl.ds(first + k, 1), :] for k in range(step)], axis=1)

        cell = row(cell_ref)
        level = jnp.bitwise_and(cell, MODES - 1)
        lon = lax.shift_right_logical(cell, 12)
        lat = jnp.bitwise_and(lax.shift_right_logical(cell, 7), CELLS - 1)
        level_hot = lax.broadcasted_iota(jnp.int32, (MODES, width), 0) == level
        level_hot = level_hot.astype(F32).astype(BF)
        level_hot = jnp.concatenate([level_hot, level_hot], axis=0)
        lon_hot = lax.broadcasted_iota(jnp.int32, (CELLS, width), 0) == lon
        lon_hot = lon_hot.astype(F32).astype(BF)
        lon_hot = jnp.concatenate([lon_hot, lon_hot], axis=0)
        mode = jnp.dot(modes_table, level_hot, preferred_element_type=F32) * row(seg_ref)
        weight = jnp.dot(lon_weights, lon_hot, preferred_element_type=F32)
        high, low = split(
            jnp.concatenate([weight[:MODES] * mode, weight[MODES:] * mode], axis=0)
        )
        lane = lax.broadcasted_iota(jnp.int32, (2 * CELLS, width), 1)
        sub = lax.broadcasted_iota(jnp.int32, (2 * CELLS, width), 0)
        lat_hot = (sub % CELLS == lat) & (sub // CELLS == (lane // SAMP) % 2)
        lat_hot = lat_hot.astype(F32).astype(BF)
        for pair in range(step // 2):
            own = slice(pair * 2 * SAMP, (pair + 1) * 2 * SAMP)
            early[part * (step // 2) + pair] = lax.dot_general(
                jnp.concatenate([lat_hot[:, own], lat_hot[:, own]], axis=1),
                jnp.concatenate([high[:, own], low[:, own]], axis=1),
                (((1,), (1,)), ((), ())),
                preferred_element_type=F32,
            )
        return 0

    lax.fori_loop(start, stop, body, 0)


def early_states(innov_rows, early, lon_state):
    for way in range(2):

        def body(part, total):
            for inner in range(4):
                innov = jnp.broadcast_to(innov_rows[pl.ds(part * 4 + inner, 1), :], (CELLS, MODES))
                sub = (inner % 2) * CELLS
                total = total + innov * early[
                    part * 2 + inner // 2, sub : sub + CELLS, way * MODES : (way + 1) * MODES
                ]
            return total

        lon_state[way] = lax.fori_loop(0, BLOCKS // 4, body, jnp.zeros((CELLS, MODES), F32))


def tile_sums(table):
    def body(cell, carried):
        grow, var, gap = carried
        decay = table[pl.ds(cell, TILES, stride=CELLS), :]
        less = 1.0 - decay
        return (
            grow * decay,
            decay * decay * var + less * jnp.sqrt(less),
            gap + grow * less,
        )

    zero = jnp.zeros((TILES, MODES), F32)
    return lax.fori_loop(0, CELLS, body, (zero + 1.0, zero, zero))


def own_tables(table, first, var, decay_ref, var_ref, enter_ref, leave_ref):
    decay_ref[...] = table[pl.ds(pl.multiple_of(first, CELLS), CELLS), :]
    grow = jnp.ones((1, MODES), F32)
    for cell in range(CELLS):
        decay = decay_ref[cell : cell + 1, :]
        less = 1.0 - decay
        var = decay * decay * var + less * jnp.sqrt(less)
        grow = grow * decay
        var_ref[cell : cell + 1, :] = var
        enter_ref[cell : cell + 1, :] = grow
    grow = jnp.ones((1, MODES), F32)
    for cell in reversed(range(CELLS)):
        leave_ref[cell : cell + 1, :] = grow * var_ref[cell : cell + 1, :]
        grow = grow * decay_ref[cell : cell + 1, :]


def kernel(
    innov_hbm, ray_hbm, cell_hbm, seg_hbm, modes_hbm, lon_hbm, lat_hbm, out_ref,
    innov_ref, ray_ref, cell_ref, seg_ref, modes_ref, lon_ref, lat_ref, in_sems,
    cells_hot, acc, field, value, innov_row, all_innov, g1_buf,
    lon_table, lat_table, lon_grow, lat_grow, chip_grow,
    lon_decay, lon_var, lon_enter, lon_leave, lat_decay, lat_var, lat_enter, lat_leave,
    lon_state, pair_buf, chip_buf, lon_carry, lat_state, lat_buf, lon_corner, lat_corner,
    smooth, early, innov_rows, lon_total, lat_total,
    g1_send, g1_recv, g2_send, g2_recv, t1_send, t1_recv, t2_send, t2_recv,
    b1_send, b1_recv, l2_send, l2_recv, pair_send, pair_recv,
):
    loads = [
        pltpu.make_async_copy(src, dst, in_sems.at[k])
        for k, (src, dst) in enumerate(
            (
                (innov_hbm, innov_ref),
                (lon_hbm, lon_ref),
                (lat_hbm, lat_ref),
                (cell_hbm, cell_ref),
                (ray_hbm, ray_ref),
                (seg_hbm, seg_ref),
                (modes_hbm, modes_ref),
            )
        )
    ]
    for load in loads:
        load.start()
    innov_in, lon_in, lat_in, *late_in = loads
    p, q = lax.axis_index("lon"), lax.axis_index("lat")
    z, core = p // 2, p % 2
    q_bits = [(q // 2**k) % 2 for k in range(4)]
    partner = p + 1 - 2 * core

    def lat_peer(mask):
        peer = q
        for k in range(4):
            if (mask >> k) & 1:
                peer = peer + (1 - 2 * q_bits[k]) * 2**k
        return peer

    def lat_slot(tile):
        slot = 0
        for k in range(4):
            bit = 1 - q_bits[k] if (tile >> k) & 1 else q_bits[k]
            slot = slot + bit * 2**k
        return slot

    def lon_peer(offset):
        return (p + offset) % TILES

    barrier = pltpu.get_barrier_semaphore()
    for offset in LON_PEERS:
        pl.semaphore_signal(
            barrier, inc=1, device_id={"lon": lon_peer(offset)}, device_id_type=MESH
        )
    for mask in LAT_PEERS:
        pl.semaphore_signal(
            barrier, inc=1, device_id={"lat": lat_peer(mask)}, device_id_type=MESH
        )

    sent = []

    def push(src, dst, send_sem, recv_sem, device):
        copy = pltpu.make_async_remote_copy(
            src_ref=src, dst_ref=dst, send_sem=send_sem, recv_sem=recv_sem,
            device_id=device, device_id_type=MESH,
        )
        copy.start()
        sent.append(copy)
        return copy

    innov_row[...] = jnp.zeros_like(innov_row)
    innov_in.wait()
    innov_row[0:1, 0:64] = innov_ref[...]
    row = jnp.broadcast_to(innov_row[0:1, :], (8, 128))
    both = row + pltpu.roll(row, 64, 1)
    sub = lax.broadcasted_iota(jnp.int32, (8, 128), 0)
    lane = lax.broadcasted_iota(jnp.int32, (8, 128), 1)
    mine = (sub == q // 2) & (lane // 64 == q % 2)
    g1_buf[0] = jnp.where(mine, both, 0.0)

    pl.semaphore_wait(barrier, 2 * (TILES - 1))
    g1 = [
        push(g1_buf.at[0], g1_buf.at[m], g1_send.at[m], g1_recv.at[m], {"lat": lat_peer(m)})
        for m in LAT_PEERS
    ]

    lon_in.wait()
    lat_in.wait()
    for part in range(4):
        span = slice(part * 128, (part + 1) * 128)
        lon_table[span, :] = lon_ref[:, span].T
        lat_table[span, :] = lat_ref[:, span].T
    grow, var, gap = tile_sums(lon_table)
    lon_grow[...] = grow
    loop, loop_gap, loop_var = grow[0:1], gap[0:1], var[0:1]
    for tile in range(1, TILES):
        own = slice(tile, tile + 1)
        loop_var = grow[own] * grow[own] * loop_var + var[own]
        loop_gap = loop_gap + loop * gap[own]
        loop = loop * grow[own]
    enter_var = loop_var / (loop_gap * (1.0 + loop))
    for tile in range(TILES - 1):
        own = slice(tile, tile + 1)
        enter_var = jnp.where(
            tile < p, grow[own] * grow[own] * enter_var + var[own], enter_var
        )
    own_tables(lon_table, p * CELLS, enter_var, lon_decay, lon_var, lon_enter, lon_leave)
    loop_scale = 1.0 / loop_gap
    for chip in range(TILES // 2):
        chip_grow[chip : chip + 1, :] = grow[2 * chip : 2 * chip + 1] * grow[2 * chip + 1 : 2 * chip + 2]

    grow, var, gap = tile_sums(lat_table)
    lat_grow[...] = grow
    enter_var = jnp.zeros((1, MODES), F32)
    for tile in range(TILES - 1):
        own = slice(tile, tile + 1)
        enter_var = jnp.where(
            tile < q, grow[own] * grow[own] * enter_var + var[own], enter_var
        )
    own_tables(lat_table, q * CELLS, enter_var, lat_decay, lat_var, lat_enter, lat_leave)

    for load in late_in:
        load.wait()
    modes_high, modes_low = split(modes_ref[...].T)
    weight_high, weight_low = split(jnp.concatenate([lon_leave[...].T, lon_enter[...].T], axis=0))
    early_tables = (
        jnp.concatenate([modes_high, modes_low], axis=1),
        jnp.concatenate([weight_high, weight_low], axis=1),
    )
    early_sums(cell_ref, seg_ref, early_tables, early, 0, 2)

    for copy in g1:
        copy.wait_recv()
    total = g1_buf[0]
    for slot in range(1, TILES):
        total = total + g1_buf[slot]
    all_innov[p] = total
    g2 = [
        push(all_innov.at[p], all_innov.at[p], g2_send.at[o], g2_recv.at[o], {"lon": lon_peer(o)})
        for o in LON_PEERS
    ]

    early_sums(cell_ref, seg_ref, early_tables, early, 2, 4)
    one_hot_rows(cell_ref, cells_hot, 0, BLOCKS)
    ray = jnp.broadcast_to(ray_ref[...].astype(F32), (BLOCKS, BLOCKS))
    diagonal = lax.broadcasted_iota(jnp.int32, (BLOCKS, BLOCKS), 0) == lax.broadcasted_iota(
        jnp.int32, (BLOCKS, BLOCKS), 1
    )
    ray = jnp.sum(jnp.where(diagonal, ray, 0.0), axis=1, keepdims=True).astype(jnp.int32)
    ray = jnp.broadcast_to(ray, (BLOCKS, 128))
    place = lax.broadcasted_iota(jnp.int32, (BLOCKS, 128), 1)
    row_hot = (place == ray // 128).astype(F32).astype(BF)
    lane_hot = place == ray % 128

    for copy in g2:
        copy.wait_recv()
    table = all_innov[...].reshape(128, 128)
    picked = jnp.zeros((BLOCKS, 128), F32)
    for _ in range(3):
        high = table.astype(BF)
        picked = picked + jnp.dot(row_hot, high, preferred_element_type=F32)
        table = table - high.astype(F32)
    picked = jnp.sum(jnp.where(lane_hot, picked, 0.0), axis=1, keepdims=True)
    innov_rows[...] = jnp.broadcast_to(picked, (BLOCKS, 128))
    early_states(innov_rows, early, lon_state)

    def corners(state):
        return [
            jnp.sum(lat_leave[...] * state, axis=0, keepdims=True),
            jnp.sum(lat_enter[...] * state, axis=0, keepdims=True),
        ]

    lon_corner[0] = jnp.concatenate(
        corners(lon_state[0]) + corners(lon_state[1]) + [jnp.zeros((4, MODES), F32)], axis=0
    )
    t1 = [
        push(lon_corner.at[0], lon_corner.at[o], t1_send.at[o], t1_recv.at[o], {"lon": lon_peer(o)})
        for o in LON_PEERS
    ]
    l1 = push(lon_state.at[1 - core], pair_buf, pair_send.at[0], pair_recv.at[0], {"lon": partner})

    value[...] = seg_ref[...] * innov_rows[...]
    scatter(cell_ref, value, cells_hot, acc, 0, 1)

    l1.wait_recv()
    chip_state = pair_buf[...] + lon_grow[pl.ds(partner, 1), :] * lon_state[core]
    chip_buf[0] = chip_state
    sign = 1 - 2 * core
    l2 = [
        push(
            chip_buf.at[0], chip_buf.at[o], l2_send.at[o], l2_recv.at[o],
            {"lon": 2 * ((z + sign * o + 8) % 8) + core},
        )
        for o in CHIP_PEERS
    ]
    scatter(cell_ref, value, cells_hot, acc, 1, 4)

    for copy in t1:
        copy.wait_recv()
    ahead = lon_corner[0]
    behind = lon_corner[0]
    for o in reversed(range(1, TILES)):
        ahead = lon_grow[pl.ds((p + TILES - o) % TILES, 1), :] * ahead + lon_corner[o]
        behind = lon_grow[pl.ds((p + o) % TILES, 1), :] * behind + lon_corner[TILES - o]
    sub = lax.broadcasted_iota(jnp.int32, (8, MODES), 0)
    lat_corner[0] = jnp.where(sub < 2, ahead, behind) * loop_scale
    t2 = [
        push(lat_corner.at[0], lat_corner.at[m], t2_send.at[m], t2_recv.at[m], {"lat": lat_peer(m)})
        for m in LAT_PEERS
    ]

    modes_high, modes_low = split(modes_ref[...])
    both = jnp.concatenate([modes_high, modes_low], axis=1)
    to_modes = jnp.concatenate([both, both], axis=0)

    def to_spectral(chunk, _):
        own = pl.ds(pl.multiple_of(chunk * 256, 256), 256)
        forcing = acc[own, 0:128] + acc[own, 128:256]
        parts = jnp.concatenate(split(forcing), axis=1)
        result = jnp.dot(parts, to_modes, preferred_element_type=F32)
        field[own, :] = result[:, 0:128] + result[:, 128:256]
        return 0

    lax.fori_loop(0, ROWS // 256, to_spectral, 0)

    def lon_rows(cell):
        return pl.ds(cell * CELLS, CELLS)

    state = jnp.zeros((CELLS, MODES), F32)
    for cell in range(CELLS):
        own = slice(cell, cell + 1)
        state = lon_decay[own] * state + lon_var[own] * field[lon_rows(cell), :]
        smooth[lon_rows(cell), :] = state
    back = jnp.zeros((CELLS, MODES), F32)
    for cell in reversed(range(CELLS)):
        own = slice(cell, cell + 1)
        whole = smooth[lon_rows(cell), :] + lon_var[own] * back
        smooth[lon_rows(cell), :] = whole
        lat_state[0, own, :] = jnp.sum(lat_leave[...] * whole, axis=0, keepdims=True)
        lat_state[1, own, :] = jnp.sum(lat_enter[...] * whole, axis=0, keepdims=True)
        back = lon_decay[own] * (back + field[lon_rows(cell), :])

    b1 = []
    for m in LAT_PEERS:
        top = m.bit_length() - 1
        b1.append(
            push(
                lat_state.at[q_bits[top]], lat_buf.at[m], b1_send.at[m], b1_recv.at[m],
                {"lat": lat_peer(m)},
            )
        )
    lat_buf[0] = lat_state[0]

    state = jnp.zeros((CELLS, MODES), F32)
    for cell in range(CELLS):
        own = slice(cell, cell + 1)
        rows = pl.ds(cell, CELLS, stride=CELLS)
        state = lat_decay[own] * state + lat_var[own] * smooth[rows, :]
        field[rows, :] = state
    back = jnp.zeros((CELLS, MODES), F32)
    for cell in reversed(range(CELLS)):
        own = slice(cell, cell + 1)
        rows = pl.ds(cell, CELLS, stride=CELLS)
        field[rows, :] = field[rows, :] + lat_var[own] * back
        back = lat_decay[own] * (back + smooth[rows, :])

    for copy in l2:
        copy.wait_recv()
    carry = chip_buf[0]
    for o in reversed(range(1, 8)):
        carry = chip_grow[pl.ds((z - sign * o + 8) % 8, 1), :] * carry + chip_buf[o]
    carry = carry * loop_scale
    lon_carry[core] = carry
    pair_buf[...] = lon_grow[pl.ds(p, 1), :] * carry + lon_state[core]
    l3 = push(pair_buf, lon_carry.at[core], pair_send.at[1], pair_recv.at[1], {"lon": partner})

    l3.wait_recv()
    for way in range(2):
        state = jnp.zeros((1, MODES), F32)
        back = jnp.zeros((1, MODES), F32)
        for cell in range(CELLS):
            own = slice(cell, cell + 1)
            state = lat_decay[own] * state + lat_var[own] * lon_carry[way, own, :]
            lon_total[way, own, :] = state
        for cell in reversed(range(CELLS)):
            own = slice(cell, cell + 1)
            lon_total[way, own, :] = lon_total[way, own, :] + lat_var[own] * back
            back = lat_decay[own] * (back + lon_carry[way, own, :])

    for copy in b1:
        copy.wait_recv()
    ahead = jnp.zeros((CELLS, MODES), F32)
    behind = jnp.zeros((CELLS, MODES), F32)
    for tile in range(TILES - 1):
        got = lat_buf[lat_slot(tile)]
        ahead = jnp.where(tile < q, lat_grow[tile : tile + 1, :] * ahead + got, ahead)
    for tile in reversed(range(1, TILES)):
        got = lat_buf[lat_slot(tile)]
        behind = jnp.where(tile > q, lat_grow[tile : tile + 1, :] * behind + got, behind)

    for copy in t2:
        copy.wait_recv()
    corner_ahead = jnp.zeros((8, MODES), F32)
    corner_behind = jnp.zeros((8, MODES), F32)
    for tile in range(TILES - 1):
        got = lat_corner[lat_slot(tile)]
        corner_ahead = jnp.where(
            tile < q, lat_grow[tile : tile + 1, :] * corner_ahead + got, corner_ahead
        )
    for tile in reversed(range(1, TILES)):
        got = lat_corner[lat_slot(tile)]
        corner_behind = jnp.where(
            tile > q, lat_grow[tile : tile + 1, :] * corner_behind + got, corner_behind
        )
    lat_total[0] = ahead + lon_enter[...] * corner_ahead[0:1] + lon_leave[...] * corner_ahead[2:3]
    lat_total[1] = behind + lon_enter[...] * corner_behind[1:2] + lon_leave[...] * corner_behind[3:4]

    both = jnp.concatenate([modes_high, modes_low], axis=0)
    to_levels = jnp.concatenate([both, both], axis=1)
    per = 8

    def to_grid(chunk, _):
        pieces = []
        for inner in range(per):
            cell = chunk * per + inner
            own = pl.ds(cell, 1)
            pieces.append(
                field[pl.ds(pl.multiple_of(cell * CELLS, CELLS), CELLS), :]
                + lon_enter[own, :] * lon_total[0]
                + lon_leave[own, :] * lon_total[1]
                + lat_enter[...] * lat_total[0, own, :]
                + lat_leave[...] * lat_total[1, own, :]
            )
        whole = jnp.concatenate(split(jnp.concatenate(pieces, axis=0)), axis=1)
        result = lax.dot_general(
            whole, to_levels, (((1,), (1,)), ((), ())), preferred_element_type=F32
        )
        own = pl.ds(pl.multiple_of(chunk * (per * CELLS), per * CELLS), per * CELLS)
        out_ref[own, :] = result[:, 0:MODES] + result[:, MODES:]
        return 0

    lax.fori_loop(0, CELLS // per, to_grid, 0)

    for copy in sent:
        copy.wait_send()


def on_device(innovation, ray_id, cell_index, seg_length, vertical_modes, lon_decay, lat_decay):
    vmem = pl.BlockSpec(memory_space=pltpu.VMEM)
    tile = lambda *shape: pltpu.VMEM(shape, F32)
    sems = lambda count: pltpu.SemaphoreType.DMA((count,))
    inputs = (
        innovation.reshape(1, 64),
        ray_id.reshape(1, BLOCKS),
        cell_index.reshape(BLOCKS, SAMP),
        seg_length.reshape(BLOCKS, SAMP),
        vertical_modes,
        lon_decay,
        lat_decay,
    )
    result = pl.pallas_call(
        kernel,
        out_shape=jax.ShapeDtypeStruct((ROWS, MODES), F32),
        in_specs=[pl.BlockSpec(memory_space=pltpu.HBM)] * 7,
        out_specs=vmem,
        scratch_shapes=[
            tile(1, 64),
            pltpu.VMEM((1, BLOCKS), jnp.int32),
            pltpu.VMEM((BLOCKS, SAMP), jnp.int32),
            tile(BLOCKS, SAMP),
            tile(MODES, MODES),
            tile(MODES, TILES * CELLS),
            tile(MODES, TILES * CELLS),
            pltpu.SemaphoreType.DMA((7,)),
            pltpu.VMEM((BLOCKS, ROWS, SAMP), BF),
            tile(ROWS, 256),
            tile(ROWS, MODES),
            tile(BLOCKS, SAMP),
            tile(8, 128),
            tile(TILES, 8, 128),
            tile(TILES, 8, 128),
            tile(TILES * CELLS, MODES),
            tile(TILES * CELLS, MODES),
            tile(TILES, MODES),
            tile(TILES, MODES),
            tile(TILES // 2, MODES),
        ]
        + [tile(CELLS, MODES)] * 8
        + [
            tile(2, CELLS, MODES),
            tile(CELLS, MODES),
            tile(8, CELLS, MODES),
            tile(2, CELLS, MODES),
            tile(2, CELLS, MODES),
            tile(TILES, CELLS, MODES),
            tile(TILES, 8, MODES),
            tile(TILES, 8, MODES),
            tile(ROWS, MODES),
            tile(BLOCKS // 2, 2 * CELLS, 2 * MODES),
            tile(BLOCKS, 128),
            tile(2, CELLS, MODES),
            tile(2, CELLS, MODES),
        ]
        + [sems(TILES)] * 10
        + [sems(8)] * 2
        + [sems(2)] * 2,
        compiler_params=pltpu.CompilerParams(
            collective_id=0, has_side_effects=True, vmem_limit_bytes=40 * 2**20
        ),
        name="covariance",
    )(*(pltpu.with_memory_space_constraint(given, pltpu.HBM) for given in inputs))
    return result.reshape(CELLS, CELLS, MODES)


def solution(mesh):
    placed = (
        P(("lon", "lat")),
        P("lon", "lat", None),
        P("lon", "lat", None, None),
        P("lon", "lat", None, None),
        P(),
        P(),
        P(),
    )
    return jax.shard_map(
        on_device, mesh=mesh, in_specs=placed, out_specs=P("lon", "lat", None), check_vma=False
    )
```

```python
import functools

import jax
import jax.numpy as jnp
from jax import lax
from jax.experimental import pallas as pl
from jax.experimental.pallas import tpu as pltpu
from jax.sharding import PartitionSpec as P

MESH = pl.DeviceIdType.MESH
BF = jnp.bfloat16
F32 = jnp.float32
CELLS = 32
TILES = 16
MODES = 128
ROWS = CELLS * CELLS
BLOCKS = 64
SAMP = 128
LAT_PEERS = (10, 2, 8, 9, 11, 6, 14, 5, 7, 13, 15, 1, 3, 4, 12)
LON_PEERS = (8, 9, 7, 6, 10, 5, 11, 4, 12, 3, 13, 2, 14, 1, 15)
CHIP_PEERS = (4, 3, 5, 2, 6, 1, 7)


def split(value):
    high = value.astype(BF)
    return high, (value - high.astype(F32)).astype(BF)


def hot(index, count):
    place = lax.broadcasted_iota(jnp.int32, (count, index.shape[1]), 0)
    return (place == index).astype(F32).astype(BF)


def lon_of(cell):
    return lax.shift_right_logical(cell, 12)


def lat_of(cell):
    return jnp.bitwise_and(lax.shift_right_logical(cell, 7), CELLS - 1)


def cell_rows(cell_ref, block):
    cell = cell_ref[pl.ds(block, 1), :]
    lat_hot = hot(lat_of(cell), CELLS)
    lon_hot = hot(lon_of(cell), CELLS).astype(F32)
    return jnp.concatenate(
        [
            lat_hot * jnp.broadcast_to(lon_hot[row : row + 1], (CELLS, SAMP)).astype(BF)
            for row in range(CELLS)
        ],
        axis=0,
    )


def valued_levels(cell_ref, value_ref, block):
    level = jnp.bitwise_and(cell_ref[pl.ds(block, 1), :], MODES - 1)
    hit = lax.broadcasted_iota(jnp.int32, (MODES, SAMP), 0) == level
    value = value_ref[pl.ds(block, 1), :]
    high = value.astype(BF).astype(F32)
    low = value - high
    return jnp.concatenate(
        [jnp.where(hit, high, 0.0).astype(BF), jnp.where(hit, low, 0.0).astype(BF)], axis=0
    )


def scatter(cell_ref, value_ref, acc, start, stop, step=16):
    if start == 0:
        acc[...] = jnp.zeros_like(acc)

    def body(chunk, _):
        total = None
        for inner in range(0, step, 2):
            block = chunk * step + inner
            levels = jnp.concatenate(
                [valued_levels(cell_ref, value_ref, block + k) for k in range(2)], axis=1
            )
            cells = jnp.concatenate([cell_rows(cell_ref, block + k) for k in range(2)], axis=1)
            part = lax.dot_general(
                cells, levels, (((1,), (1,)), ((), ())), preferred_element_type=F32
            )
            total = part if total is None else total + part
        acc[...] += total
        return 0

    lax.fori_loop(start, stop, body, 0)


def early_sums(cell_ref, seg_ref, tables, early_lon, early_lat, start, stop, step=8):
    modes_table, lon_weights, lat_weights = tables

    def body(part, _):
        first = part * step

        def row(ref):
            return jnp.concatenate([ref[pl.ds(first + k, 1), :] for k in range(step)], axis=1)

        def twice(value, axis):
            return jnp.concatenate([value, value], axis=axis)

        cell = row(cell_ref)
        level_hot = twice(hot(jnp.bitwise_and(cell, MODES - 1), MODES), 0)
        lon_hot = hot(lon_of(cell), CELLS)
        lat_hot = hot(lat_of(cell), CELLS)
        mode = jnp.dot(modes_table, level_hot, preferred_element_type=F32) * row(seg_ref)

        def sums(weights, summed, kept, early):
            weight = jnp.dot(weights, twice(summed, 0), preferred_element_type=F32)
            high, low = split(
                jnp.concatenate([weight[:MODES] * mode, weight[MODES:] * mode], axis=0)
            )
            for inner in range(step):
                own = slice(inner * SAMP, (inner + 1) * SAMP)
                early[first + inner] = lax.dot_general(
                    twice(kept[:, own], 1),
                    jnp.concatenate([high[:, own], low[:, own]], axis=1),
                    (((1,), (1,)), ((), ())),
                    preferred_element_type=F32,
                )

        sums(lon_weights, lon_hot, lat_hot, early_lon)
        sums(lat_weights, lat_hot, lon_hot, early_lat)
        return 0

    lax.fori_loop(start, stop, body, 0)


def early_states(innov_rows, early, states):
    for way in range(2):

        def body(part, total):
            for inner in range(4):
                block = part * 4 + inner
                innov = jnp.broadcast_to(innov_rows[pl.ds(block, 1), :], (CELLS, MODES))
                total = total + innov * early[block, :, way * MODES : (way + 1) * MODES]
            return total

        states[way] = lax.fori_loop(0, BLOCKS // 4, body, jnp.zeros((CELLS, MODES), F32))


def row_filter(decay, var, given, result):
    for way in range(2):
        state = jnp.zeros((1, MODES), F32)
        back = jnp.zeros((1, MODES), F32)
        for cell in range(CELLS):
            own = slice(cell, cell + 1)
            state = decay[own] * state + var[own] * given[way, own, :]
            result[way, own, :] = state
        for cell in reversed(range(CELLS)):
            own = slice(cell, cell + 1)
            result[way, own, :] = result[way, own, :] + var[own] * back
            back = decay[own] * (back + given[way, own, :])


def tile_sums(table):
    def body(cell, carried):
        grow, var, gap = carried
        decay = table[pl.ds(cell, TILES, stride=CELLS), :]
        less = 1.0 - decay
        return (
            grow * decay,
            decay * decay * var + less * jnp.sqrt(less),
            gap + grow * less,
        )

    zero = jnp.zeros((TILES, MODES), F32)
    return lax.fori_loop(0, CELLS, body, (zero + 1.0, zero, zero))


def own_tables(table, first, var, decay_ref, var_ref, enter_ref, leave_ref):
    decay_ref[...] = table[pl.ds(pl.multiple_of(first, CELLS), CELLS), :]
    grow = jnp.ones((1, MODES), F32)
    for cell in range(CELLS):
        decay = decay_ref[cell : cell + 1, :]
        less = 1.0 - decay
        var = decay * decay * var + less * jnp.sqrt(less)
        grow = grow * decay
        var_ref[cell : cell + 1, :] = var
        enter_ref[cell : cell + 1, :] = grow
    grow = jnp.ones((1, MODES), F32)
    for cell in reversed(range(CELLS)):
        leave_ref[cell : cell + 1, :] = grow * var_ref[cell : cell + 1, :]
        grow = grow * decay_ref[cell : cell + 1, :]


def kernel(
    innov_hbm, ray_hbm, cell_hbm, seg_hbm, modes_hbm, lon_hbm, lat_hbm, out_ref,
    innov_ref, ray_ref, cell_ref, seg_ref, modes_ref, lon_ref, lat_ref, in_sems,
    acc, field, value, innov_row, all_innov, g1_buf,
    lon_table, lat_table, lon_grow, lat_grow, chip_grow,
    lon_decay, lon_var, lon_enter, lon_leave, lat_decay, lat_var, lat_enter, lat_leave,
    lon_state, pair_buf, chip_buf, lon_carry, lat_state, lat_buf, lon_corner, lat_corner,
    smooth, early_lon, early_lat, innov_rows, lon_total, lat_total, lat_carry,
    g1_send, g1_recv, g2_send, g2_recv, t1_send, t1_recv, t2_send, t2_recv,
    b1_send, b1_recv, l2_send, l2_recv, pair_send, pair_recv,
):
    loads = [
        pltpu.make_async_copy(src, dst, in_sems.at[k])
        for k, (src, dst) in enumerate(
            (
                (innov_hbm, innov_ref),
                (lon_hbm, lon_ref),
                (lat_hbm, lat_ref),
                (cell_hbm, cell_ref),
                (ray_hbm, ray_ref),
                (seg_hbm, seg_ref),
                (modes_hbm, modes_ref),
            )
        )
    ]
    for load in loads:
        load.start()
    innov_in, lon_in, lat_in, *late_in = loads
    p, q = lax.axis_index("lon"), lax.axis_index("lat")
    z, core = p // 2, p % 2
    q_bits = [(q // 2**k) % 2 for k in range(4)]
    partner = p + 1 - 2 * core

    def lat_peer(mask):
        peer = q
        for k in range(4):
            if (mask >> k) & 1:
                peer = peer + (1 - 2 * q_bits[k]) * 2**k
        return peer

    def lat_slot(tile):
        slot = 0
        for k in range(4):
            bit = 1 - q_bits[k] if (tile >> k) & 1 else q_bits[k]
            slot = slot + bit * 2**k
        return slot

    def lon_peer(offset):
        return (p + offset) % TILES

    barrier = pltpu.get_barrier_semaphore()
    for offset in LON_PEERS:
        pl.semaphore_signal(
            barrier, inc=1, device_id={"lon": lon_peer(offset)}, device_id_type=MESH
        )
    for mask in LAT_PEERS:
        pl.semaphore_signal(
            barrier, inc=1, device_id={"lat": lat_peer(mask)}, device_id_type=MESH
        )

    sent = []

    def push(src, dst, send_sem, recv_sem, device):
        copy = pltpu.make_async_remote_copy(
            src_ref=src, dst_ref=dst, send_sem=send_sem, recv_sem=recv_sem,
            device_id=device, device_id_type=MESH,
        )
        copy.start()
        sent.append(copy)
        return copy

    innov_row[...] = jnp.zeros_like(innov_row)
    innov_in.wait()
    innov_row[0:1, 0:64] = innov_ref[...]
    row = jnp.broadcast_to(innov_row[0:1, :], (8, 128))
    both = row + pltpu.roll(row, 64, 1)
    sub = lax.broadcasted_iota(jnp.int32, (8, 128), 0)
    lane = lax.broadcasted_iota(jnp.int32, (8, 128), 1)
    mine = (sub == q // 2) & (lane // 64 == q % 2)
    g1_buf[0] = jnp.where(mine, both, 0.0)

    lon_in.wait()
    lat_in.wait()
    for part in range(4):
        span = slice(part * 128, (part + 1) * 128)
        lon_table[span, :] = lon_ref[:, span].T
        lat_table[span, :] = lat_ref[:, span].T
    grow, var, gap = tile_sums(lon_table)
    lon_grow[...] = grow
    loop, loop_gap, loop_var = grow[0:1], gap[0:1], var[0:1]
    for tile in range(1, TILES):
        own = slice(tile, tile + 1)
        loop_var = grow[own] * grow[own] * loop_var + var[own]
        loop_gap = loop_gap + loop * gap[own]
        loop = loop * grow[own]
    enter_var = loop_var / (loop_gap * (1.0 + loop))
    for tile in range(TILES - 1):
        own = slice(tile, tile + 1)
        enter_var = jnp.where(
            tile < p, grow[own] * grow[own] * enter_var + var[own], enter_var
        )
    own_tables(lon_table, p * CELLS, enter_var, lon_decay, lon_var, lon_enter, lon_leave)
    loop_scale = 1.0 / loop_gap
    for chip in range(TILES // 2):
        chip_grow[chip : chip + 1, :] = grow[2 * chip : 2 * chip + 1] * grow[2 * chip + 1 : 2 * chip + 2]

    grow, var, gap = tile_sums(lat_table)
    lat_grow[...] = grow
    enter_var = jnp.zeros((1, MODES), F32)
    for tile in range(TILES - 1):
        own = slice(tile, tile + 1)
        enter_var = jnp.where(
            tile < q, grow[own] * grow[own] * enter_var + var[own], enter_var
        )
    own_tables(lat_table, q * CELLS, enter_var, lat_decay, lat_var, lat_enter, lat_leave)

    pl.semaphore_wait(barrier, 2 * (TILES - 1))
    g1 = [
        push(g1_buf.at[0], g1_buf.at[m], g1_send.at[m], g1_recv.at[m], {"lat": lat_peer(m)})
        for m in LAT_PEERS
    ]

    for load in late_in:
        load.wait()
    modes_high, modes_low = split(modes_ref[...].T)

    def weight_table(leave, enter):
        return jnp.concatenate(
            split(jnp.concatenate([leave[...].T, enter[...].T], axis=0)), axis=1
        )

    early_tables = (
        jnp.concatenate([modes_high, modes_low], axis=1),
        weight_table(lon_leave, lon_enter),
        weight_table(lat_leave, lat_enter),
    )
    early_sums(cell_ref, seg_ref, early_tables, early_lon, early_lat, 0, 4)

    for copy in g1:
        copy.wait_recv()
    total = g1_buf[0]
    for slot in range(1, TILES):
        total = total + g1_buf[slot]
    all_innov[p] = total
    g2 = [
        push(all_innov.at[p], all_innov.at[p], g2_send.at[o], g2_recv.at[o], {"lon": lon_peer(o)})
        for o in LON_PEERS
    ]

    early_sums(cell_ref, seg_ref, early_tables, early_lon, early_lat, 4, 8)
    ray = jnp.broadcast_to(ray_ref[...].astype(F32), (BLOCKS, BLOCKS))
    diagonal = lax.broadcasted_iota(jnp.int32, (BLOCKS, BLOCKS), 0) == lax.broadcasted_iota(
        jnp.int32, (BLOCKS, BLOCKS), 1
    )
    ray = jnp.sum(jnp.where(diagonal, ray, 0.0), axis=1, keepdims=True).astype(jnp.int32)
    ray = jnp.broadcast_to(ray, (BLOCKS, 128))
    place = lax.broadcasted_iota(jnp.int32, (BLOCKS, 128), 1)
    row_hot = (place == ray // 128).astype(F32).astype(BF)
    lane_hot = place == ray % 128

    for copy in g2:
        copy.wait_recv()
    table = all_innov[...].reshape(128, 128)
    picked = jnp.zeros((BLOCKS, 128), F32)
    for _ in range(3):
        high = table.astype(BF)
        picked = picked + jnp.dot(row_hot, high, preferred_element_type=F32)
        table = table - high.astype(F32)
    picked = jnp.sum(jnp.where(lane_hot, picked, 0.0), axis=1, keepdims=True)
    innov_rows[...] = jnp.broadcast_to(picked, (BLOCKS, 128))
    early_states(innov_rows, early_lon, lon_state)

    def corners(state):
        return [
            jnp.sum(lat_leave[...] * state, axis=0, keepdims=True),
            jnp.sum(lat_enter[...] * state, axis=0, keepdims=True),
        ]

    lon_corner[0] = jnp.concatenate(
        corners(lon_state[0]) + corners(lon_state[1]) + [jnp.zeros((4, MODES), F32)], axis=0
    )
    t1 = [
        push(lon_corner.at[0], lon_corner.at[o], t1_send.at[o], t1_recv.at[o], {"lon": lon_peer(o)})
        for o in LON_PEERS
    ]
    l1 = push(lon_state.at[1 - core], pair_buf, pair_send.at[0], pair_recv.at[0], {"lon": partner})

    early_states(innov_rows, early_lat, lat_state)
    b1 = []
    for m in LAT_PEERS:
        top = m.bit_length() - 1
        b1.append(
            push(
                lat_state.at[q_bits[top]], lat_buf.at[m], b1_send.at[m], b1_recv.at[m],
                {"lat": lat_peer(m)},
            )
        )
    lat_buf[0] = lat_state[0]

    value[...] = seg_ref[...] * innov_rows[...]
    scatter(cell_ref, value, acc, 0, 1)

    l1.wait_recv()
    chip_state = pair_buf[...] + lon_grow[pl.ds(partner, 1), :] * lon_state[core]
    chip_buf[0] = chip_state
    sign = 1 - 2 * core
    l2 = [
        push(
            chip_buf.at[0], chip_buf.at[o], l2_send.at[o], l2_recv.at[o],
            {"lon": 2 * ((z + sign * o + 8) % 8) + core},
        )
        for o in CHIP_PEERS
    ]
    scatter(cell_ref, value, acc, 1, 3)

    for copy in t1:
        copy.wait_recv()
    ahead = lon_corner[0]
    behind = lon_corner[0]
    for o in reversed(range(1, TILES)):
        ahead = lon_grow[pl.ds((p + TILES - o) % TILES, 1), :] * ahead + lon_corner[o]
        behind = lon_grow[pl.ds((p + o) % TILES, 1), :] * behind + lon_corner[TILES - o]
    sub = lax.broadcasted_iota(jnp.int32, (8, MODES), 0)
    lat_corner[0] = jnp.where(sub < 2, ahead, behind) * loop_scale
    t2 = [
        push(lat_corner.at[0], lat_corner.at[m], t2_send.at[m], t2_recv.at[m], {"lat": lat_peer(m)})
        for m in LAT_PEERS
    ]

    scatter(cell_ref, value, acc, 3, 4)

    modes_high, modes_low = split(modes_ref[...])
    both = jnp.concatenate([modes_high, modes_low], axis=1)
    to_modes = jnp.concatenate([both, both], axis=0)

    for chunk in range(ROWS // 256):
        own = slice(chunk * 256, (chunk + 1) * 256)
        forcing = acc[own, 0:128] + acc[own, 128:256]
        parts = jnp.concatenate(split(forcing), axis=1)
        result = jnp.dot(parts, to_modes, preferred_element_type=F32)
        field[own, :] = result[:, 0:128] + result[:, 128:256]

    def lon_rows(cell):
        return pl.ds(cell * CELLS, CELLS)

    state = jnp.zeros((CELLS, MODES), F32)
    for cell in range(CELLS):
        own = slice(cell, cell + 1)
        state = lon_decay[own] * state + lon_var[own] * field[lon_rows(cell), :]
        smooth[lon_rows(cell), :] = state
    back = jnp.zeros((CELLS, MODES), F32)
    for cell in reversed(range(CELLS)):
        own = slice(cell, cell + 1)
        smooth[lon_rows(cell), :] = smooth[lon_rows(cell), :] + lon_var[own] * back
        back = lon_decay[own] * (back + field[lon_rows(cell), :])

    state = jnp.zeros((CELLS, MODES), F32)
    for cell in range(CELLS):
        own = slice(cell, cell + 1)
        rows = pl.ds(cell, CELLS, stride=CELLS)
        state = lat_decay[own] * state + lat_var[own] * smooth[rows, :]
        field[rows, :] = state
    back = jnp.zeros((CELLS, MODES), F32)
    for cell in reversed(range(CELLS)):
        own = slice(cell, cell + 1)
        rows = pl.ds(cell, CELLS, stride=CELLS)
        field[rows, :] = field[rows, :] + lat_var[own] * back
        back = lat_decay[own] * (back + smooth[rows, :])

    for copy in l2:
        copy.wait_recv()
    carry = chip_buf[0]
    for o in reversed(range(1, 8)):
        carry = chip_grow[pl.ds((z - sign * o + 8) % 8, 1), :] * carry + chip_buf[o]
    carry = carry * loop_scale
    lon_carry[core] = carry
    pair_buf[...] = lon_grow[pl.ds(p, 1), :] * carry + lon_state[core]
    l3 = push(pair_buf, lon_carry.at[core], pair_send.at[1], pair_recv.at[1], {"lon": partner})

    l3.wait_recv()
    row_filter(lat_decay, lat_var, lon_carry, lon_total)

    for copy in b1:
        copy.wait_recv()
    ahead = jnp.zeros((CELLS, MODES), F32)
    behind = jnp.zeros((CELLS, MODES), F32)
    for tile in range(TILES - 1):
        got = lat_buf[lat_slot(tile)]
        ahead = jnp.where(tile < q, lat_grow[tile : tile + 1, :] * ahead + got, ahead)
    for tile in reversed(range(1, TILES)):
        got = lat_buf[lat_slot(tile)]
        behind = jnp.where(tile > q, lat_grow[tile : tile + 1, :] * behind + got, behind)

    lat_carry[0] = ahead
    lat_carry[1] = behind
    row_filter(lon_decay, lon_var, lat_carry, lat_total)

    for copy in t2:
        copy.wait_recv()
    corner_ahead = jnp.zeros((8, MODES), F32)
    corner_behind = jnp.zeros((8, MODES), F32)
    for tile in range(TILES - 1):
        got = lat_corner[lat_slot(tile)]
        corner_ahead = jnp.where(
            tile < q, lat_grow[tile : tile + 1, :] * corner_ahead + got, corner_ahead
        )
    for tile in reversed(range(1, TILES)):
        got = lat_corner[lat_slot(tile)]
        corner_behind = jnp.where(
            tile > q, lat_grow[tile : tile + 1, :] * corner_behind + got, corner_behind
        )
    lat_total[0] += lon_enter[...] * corner_ahead[0:1] + lon_leave[...] * corner_ahead[2:3]
    lat_total[1] += lon_enter[...] * corner_behind[1:2] + lon_leave[...] * corner_behind[3:4]

    both = jnp.concatenate([modes_high, modes_low], axis=0)
    to_levels = jnp.concatenate([both, both], axis=1)
    per = 8
    for chunk in range(CELLS // per):
        pieces = []
        for cell in range(chunk * per, (chunk + 1) * per):
            own = slice(cell, cell + 1)
            pieces.append(
                field[lon_rows(cell), :]
                + lon_enter[own, :] * lon_total[0]
                + lon_leave[own, :] * lon_total[1]
                + lat_enter[...] * lat_total[0, own, :]
                + lat_leave[...] * lat_total[1, own, :]
            )
        whole = jnp.concatenate(split(jnp.concatenate(pieces, axis=0)), axis=1)
        result = lax.dot_general(
            whole, to_levels, (((1,), (1,)), ((), ())), preferred_element_type=F32
        )
        own = slice(chunk * per * CELLS, (chunk + 1) * per * CELLS)
        out_ref[own, :] = result[:, 0:MODES] + result[:, MODES:]

    for copy in sent:
        copy.wait_send()


def on_device(innovation, ray_id, cell_index, seg_length, vertical_modes, lon_decay, lat_decay):
    vmem = pl.BlockSpec(memory_space=pltpu.VMEM)
    tile = lambda *shape: pltpu.VMEM(shape, F32)
    sems = lambda count: pltpu.SemaphoreType.DMA((count,))
    inputs = (
        innovation.reshape(1, 64),
        ray_id.reshape(1, BLOCKS),
        cell_index.reshape(BLOCKS, SAMP),
        seg_length.reshape(BLOCKS, SAMP),
        vertical_modes,
        lon_decay,
        lat_decay,
    )
    result = pl.pallas_call(
        kernel,
        out_shape=jax.ShapeDtypeStruct((ROWS, MODES), F32),
        in_specs=[pl.BlockSpec(memory_space=pltpu.HBM)] * 7,
        out_specs=vmem,
        scratch_shapes=[
            tile(1, 64),
            pltpu.VMEM((1, BLOCKS), jnp.int32),
            pltpu.VMEM((BLOCKS, SAMP), jnp.int32),
            tile(BLOCKS, SAMP),
            tile(MODES, MODES),
            tile(MODES, TILES * CELLS),
            tile(MODES, TILES * CELLS),
            pltpu.SemaphoreType.DMA((7,)),
            tile(ROWS, 256),
            tile(ROWS, MODES),
            tile(BLOCKS, SAMP),
            tile(8, 128),
            tile(TILES, 8, 128),
            tile(TILES, 8, 128),
            tile(TILES * CELLS, MODES),
            tile(TILES * CELLS, MODES),
            tile(TILES, MODES),
            tile(TILES, MODES),
            tile(TILES // 2, MODES),
        ]
        + [tile(CELLS, MODES)] * 8
        + [
            tile(2, CELLS, MODES),
            tile(CELLS, MODES),
            tile(8, CELLS, MODES),
            tile(2, CELLS, MODES),
            tile(2, CELLS, MODES),
            tile(TILES, CELLS, MODES),
            tile(TILES, 8, MODES),
            tile(TILES, 8, MODES),
            tile(ROWS, MODES),
            tile(BLOCKS, CELLS, 2 * MODES),
            tile(BLOCKS, CELLS, 2 * MODES),
            tile(BLOCKS, 128),
            tile(2, CELLS, MODES),
            tile(2, CELLS, MODES),
            tile(2, CELLS, MODES),
        ]
        + [sems(TILES)] * 10
        + [sems(8)] * 2
        + [sems(2)] * 2,
        compiler_params=pltpu.CompilerParams(
            collective_id=0, has_side_effects=True, vmem_limit_bytes=40 * 2**20
        ),
        name="covariance",
    )(*(pltpu.with_memory_space_constraint(given, pltpu.HBM) for given in inputs))
    return result.reshape(CELLS, CELLS, MODES)


def solution(mesh):
    placed = (
        P(("lon", "lat")),
        P("lon", "lat", None),
        P("lon", "lat", None, None),
        P("lon", "lat", None, None),
        P(),
        P(),
        P(),
    )
    return jax.shard_map(
        on_device, mesh=mesh, in_specs=placed, out_specs=P("lon", "lat", None), check_vma=False
    )
```

```python
import functools

import jax
import jax.numpy as jnp
from jax import lax
from jax.experimental import pallas as pl
from jax.experimental.pallas import tpu as pltpu
from jax.sharding import PartitionSpec as P

MESH = pl.DeviceIdType.MESH
BF = jnp.bfloat16
F32 = jnp.float32
CELLS = 32
TILES = 16
MODES = 128
ROWS = CELLS * CELLS
BLOCKS = 64
SAMP = 128
LAT_PEERS = (10, 2, 8, 9, 11, 6, 14, 5, 7, 13, 15, 1, 3, 4, 12)
LON_PEERS = (8, 9, 7, 6, 10, 5, 11, 4, 12, 3, 13, 2, 14, 1, 15)
CHIP_PEERS = (4, 3, 5, 2, 6, 1, 7)


def split(value):
    high = value.astype(BF)
    return high, (value - high.astype(F32)).astype(BF)


def hot(index, count):
    place = lax.broadcasted_iota(jnp.int32, (count, index.shape[1]), 0)
    return (place == index).astype(F32).astype(BF)


def lon_of(cell):
    return lax.shift_right_logical(cell, 12)


def lat_of(cell):
    return jnp.bitwise_and(lax.shift_right_logical(cell, 7), CELLS - 1)


def cell_rows(cell_ref, block):
    cell = cell_ref[pl.ds(block, 1), :]
    lat_hot = hot(lat_of(cell), CELLS)
    lon_hot = hot(lon_of(cell), CELLS).astype(F32)
    return jnp.concatenate(
        [
            lat_hot * jnp.broadcast_to(lon_hot[row : row + 1], (CELLS, SAMP)).astype(BF)
            for row in range(CELLS)
        ],
        axis=0,
    )


def valued_levels(cell_ref, value_ref, block):
    level = jnp.bitwise_and(cell_ref[pl.ds(block, 1), :], MODES - 1)
    hit = lax.broadcasted_iota(jnp.int32, (MODES, SAMP), 0) == level
    value = value_ref[pl.ds(block, 1), :]
    high = value.astype(BF).astype(F32)
    low = value - high
    return jnp.concatenate(
        [jnp.where(hit, high, 0.0).astype(BF), jnp.where(hit, low, 0.0).astype(BF)], axis=0
    )


def scatter(cell_ref, value_ref, acc, start, stop, step=16):
    if start == 0:
        acc[...] = jnp.zeros_like(acc)

    def body(chunk, _):
        total = None
        for inner in range(0, step, 2):
            block = chunk * step + inner
            levels = jnp.concatenate(
                [valued_levels(cell_ref, value_ref, block + k) for k in range(2)], axis=1
            )
            cells = jnp.concatenate([cell_rows(cell_ref, block + k) for k in range(2)], axis=1)
            part = lax.dot_general(
                cells, levels, (((1,), (1,)), ((), ())), preferred_element_type=F32
            )
            total = part if total is None else total + part
        acc[...] += total
        return 0

    lax.fori_loop(start, stop, body, 0)


def early_sums(cell_ref, seg_ref, tables, early_lon, early_lat, start, stop, step=16):
    modes_table, lon_weights, lat_weights = tables

    def body(part, _):
        first = part * step

        def row(ref):
            return jnp.concatenate([ref[pl.ds(first + k, 1), :] for k in range(step)], axis=1)

        def twice(value, axis):
            return jnp.concatenate([value, value], axis=axis)

        cell = row(cell_ref)
        level_hot = twice(hot(jnp.bitwise_and(cell, MODES - 1), MODES), 0)
        lon_hot = hot(lon_of(cell), CELLS)
        lat_hot = hot(lat_of(cell), CELLS)
        mode = jnp.dot(modes_table, level_hot, preferred_element_type=F32) * row(seg_ref)

        def sums(weights, summed, kept, early):
            weight = jnp.dot(weights, twice(summed, 0), preferred_element_type=F32)
            high, low = split(
                jnp.concatenate([weight[:MODES] * mode, weight[MODES:] * mode], axis=0)
            )
            for inner in range(step):
                own = slice(inner * SAMP, (inner + 1) * SAMP)
                early[first + inner] = lax.dot_general(
                    twice(kept[:, own], 1),
                    jnp.concatenate([high[:, own], low[:, own]], axis=1),
                    (((1,), (1,)), ((), ())),
                    preferred_element_type=F32,
                )

        sums(lon_weights, lon_hot, lat_hot, early_lon)
        sums(lat_weights, lat_hot, lon_hot, early_lat)
        return 0

    lax.fori_loop(start, stop, body, 0)


def early_states(innov_rows, early, states):
    for way in range(2):

        def body(part, total):
            for inner in range(4):
                block = part * 4 + inner
                innov = jnp.broadcast_to(innov_rows[pl.ds(block, 1), :], (CELLS, MODES))
                total = total + innov * early[block, :, way * MODES : (way + 1) * MODES]
            return total

        states[way] = lax.fori_loop(0, BLOCKS // 4, body, jnp.zeros((CELLS, MODES), F32))


def row_filter(decay, var, given, result):
    for way in range(2):
        state = jnp.zeros((1, MODES), F32)
        back = jnp.zeros((1, MODES), F32)
        for cell in range(CELLS):
            own = slice(cell, cell + 1)
            state = decay[own] * state + var[own] * given[way, own, :]
            result[way, own, :] = state
        for cell in reversed(range(CELLS)):
            own = slice(cell, cell + 1)
            result[way, own, :] = result[way, own, :] + var[own] * back
            back = decay[own] * (back + given[way, own, :])


def tile_sums(table):
    def body(cell, carried):
        grow, var, gap = carried
        decay = table[pl.ds(cell, TILES, stride=CELLS), :]
        less = 1.0 - decay
        return (
            grow * decay,
            decay * decay * var + less * jnp.sqrt(less),
            gap + grow * less,
        )

    zero = jnp.zeros((TILES, MODES), F32)
    return lax.fori_loop(0, CELLS, body, (zero + 1.0, zero, zero))


def own_tables(table, first, var, decay_ref, var_ref, enter_ref, leave_ref):
    decay_ref[...] = table[pl.ds(pl.multiple_of(first, CELLS), CELLS), :]
    grow = jnp.ones((1, MODES), F32)
    for cell in range(CELLS):
        decay = decay_ref[cell : cell + 1, :]
        less = 1.0 - decay
        var = decay * decay * var + less * jnp.sqrt(less)
        grow = grow * decay
        var_ref[cell : cell + 1, :] = var
        enter_ref[cell : cell + 1, :] = grow
    grow = jnp.ones((1, MODES), F32)
    for cell in reversed(range(CELLS)):
        leave_ref[cell : cell + 1, :] = grow * var_ref[cell : cell + 1, :]
        grow = grow * decay_ref[cell : cell + 1, :]


def kernel(
    innov_hbm, ray_hbm, cell_hbm, seg_hbm, modes_hbm, lon_hbm, lat_hbm, out_ref,
    innov_ref, ray_ref, cell_ref, seg_ref, modes_ref, lon_ref, lat_ref, in_sems,
    acc, field, value, innov_row, all_innov, g1_buf,
    lon_table, lat_table, lon_grow, lat_grow, chip_grow,
    lon_decay, lon_var, lon_enter, lon_leave, lat_decay, lat_var, lat_enter, lat_leave,
    lon_state, pair_buf, chip_buf, lon_carry, lat_state, lat_buf, lon_corner, lat_corner,
    smooth, early_lon, early_lat, innov_rows, lon_total, lat_total, lat_carry,
    g1_send, g1_recv, g2_send, g2_recv, t1_send, t1_recv, t2_send, t2_recv,
    b1_send, b1_recv, l2_send, l2_recv, pair_send, pair_recv,
):
    loads = [
        pltpu.make_async_copy(src, dst, in_sems.at[k])
        for k, (src, dst) in enumerate(
            (
                (innov_hbm, innov_ref),
                (lon_hbm, lon_ref),
                (lat_hbm, lat_ref),
                (cell_hbm, cell_ref),
                (ray_hbm, ray_ref),
                (seg_hbm, seg_ref),
                (modes_hbm, modes_ref),
            )
        )
    ]
    for load in loads:
        load.start()
    innov_in, lon_in, lat_in, *late_in = loads
    p, q = lax.axis_index("lon"), lax.axis_index("lat")
    z, core = p // 2, p % 2
    q_bits = [(q // 2**k) % 2 for k in range(4)]
    partner = p + 1 - 2 * core

    def lat_peer(mask):
        peer = q
        for k in range(4):
            if (mask >> k) & 1:
                peer = peer + (1 - 2 * q_bits[k]) * 2**k
        return peer

    def lat_slot(tile):
        slot = 0
        for k in range(4):
            bit = 1 - q_bits[k] if (tile >> k) & 1 else q_bits[k]
            slot = slot + bit * 2**k
        return slot

    def lon_peer(offset):
        return (p + offset) % TILES

    barrier = pltpu.get_barrier_semaphore()
    for offset in LON_PEERS:
        pl.semaphore_signal(
            barrier, inc=1, device_id={"lon": lon_peer(offset)}, device_id_type=MESH
        )
    for mask in LAT_PEERS:
        pl.semaphore_signal(
            barrier, inc=1, device_id={"lat": lat_peer(mask)}, device_id_type=MESH
        )

    sent = []

    def push(src, dst, send_sem, recv_sem, device):
        copy = pltpu.make_async_remote_copy(
            src_ref=src, dst_ref=dst, send_sem=send_sem, recv_sem=recv_sem,
            device_id=device, device_id_type=MESH,
        )
        copy.start()
        sent.append(copy)
        return copy

    innov_row[...] = jnp.zeros_like(innov_row)
    innov_in.wait()
    innov_row[0:1, 0:64] = innov_ref[...]
    row = jnp.broadcast_to(innov_row[0:1, :], (8, 128))
    both = row + pltpu.roll(row, 64, 1)
    sub = lax.broadcasted_iota(jnp.int32, (8, 128), 0)
    lane = lax.broadcasted_iota(jnp.int32, (8, 128), 1)
    mine = (sub == q // 2) & (lane // 64 == q % 2)
    g1_buf[0] = jnp.where(mine, both, 0.0)

    lon_in.wait()
    lat_in.wait()
    for part in range(4):
        span = slice(part * 128, (part + 1) * 128)
        lon_table[span, :] = lon_ref[:, span].T
        lat_table[span, :] = lat_ref[:, span].T
    grow, var, gap = tile_sums(lon_table)
    lon_grow[...] = grow
    loop, loop_gap, loop_var = grow[0:1], gap[0:1], var[0:1]
    for tile in range(1, TILES):
        own = slice(tile, tile + 1)
        loop_var = grow[own] * grow[own] * loop_var + var[own]
        loop_gap = loop_gap + loop * gap[own]
        loop = loop * grow[own]
    enter_var = loop_var / (loop_gap * (1.0 + loop))
    for tile in range(TILES - 1):
        own = slice(tile, tile + 1)
        enter_var = jnp.where(
            tile < p, grow[own] * grow[own] * enter_var + var[own], enter_var
        )
    own_tables(lon_table, p * CELLS, enter_var, lon_decay, lon_var, lon_enter, lon_leave)
    loop_scale = 1.0 / loop_gap
    for chip in range(TILES // 2):
        chip_grow[chip : chip + 1, :] = grow[2 * chip : 2 * chip + 1] * grow[2 * chip + 1 : 2 * chip + 2]

    grow, var, gap = tile_sums(lat_table)
    lat_grow[...] = grow
    enter_var = jnp.zeros((1, MODES), F32)
    for tile in range(TILES - 1):
        own = slice(tile, tile + 1)
        enter_var = jnp.where(
            tile < q, grow[own] * grow[own] * enter_var + var[own], enter_var
        )
    own_tables(lat_table, q * CELLS, enter_var, lat_decay, lat_var, lat_enter, lat_leave)

    for load in late_in:
        load.wait()
    modes_high, modes_low = split(modes_ref[...].T)

    def weight_table(leave, enter):
        return jnp.concatenate(
            split(jnp.concatenate([leave[...].T, enter[...].T], axis=0)), axis=1
        )

    early_tables = (
        jnp.concatenate([modes_high, modes_low], axis=1),
        weight_table(lon_leave, lon_enter),
        weight_table(lat_leave, lat_enter),
    )
    pl.semaphore_wait(barrier, 2 * (TILES - 1))
    g1 = [
        push(g1_buf.at[0], g1_buf.at[m], g1_send.at[m], g1_recv.at[m], {"lat": lat_peer(m)})
        for m in LAT_PEERS
    ]

    early_sums(cell_ref, seg_ref, early_tables, early_lon, early_lat, 0, 2)

    for copy in g1:
        copy.wait_recv()
    total = g1_buf[0]
    for slot in range(1, TILES):
        total = total + g1_buf[slot]
    all_innov[p] = total
    g2 = [
        push(all_innov.at[p], all_innov.at[p], g2_send.at[o], g2_recv.at[o], {"lon": lon_peer(o)})
        for o in LON_PEERS
    ]

    early_sums(cell_ref, seg_ref, early_tables, early_lon, early_lat, 2, 4)
    ray = jnp.broadcast_to(ray_ref[...].astype(F32), (BLOCKS, BLOCKS))
    diagonal = lax.broadcasted_iota(jnp.int32, (BLOCKS, BLOCKS), 0) == lax.broadcasted_iota(
        jnp.int32, (BLOCKS, BLOCKS), 1
    )
    ray = jnp.sum(jnp.where(diagonal, ray, 0.0), axis=1, keepdims=True).astype(jnp.int32)
    ray = jnp.broadcast_to(ray, (BLOCKS, 128))
    place = lax.broadcasted_iota(jnp.int32, (BLOCKS, 128), 1)
    row_hot = (place == ray // 128).astype(F32).astype(BF)
    lane_hot = place == ray % 128

    for copy in g2:
        copy.wait_recv()
    table = all_innov[...].reshape(128, 128)
    picked = jnp.zeros((BLOCKS, 128), F32)
    for _ in range(3):
        high = table.astype(BF)
        picked = picked + jnp.dot(row_hot, high, preferred_element_type=F32)
        table = table - high.astype(F32)
    picked = jnp.sum(jnp.where(lane_hot, picked, 0.0), axis=1, keepdims=True)
    innov_rows[...] = jnp.broadcast_to(picked, (BLOCKS, 128))
    early_states(innov_rows, early_lon, lon_state)

    def corners(state):
        return [
            jnp.sum(lat_leave[...] * state, axis=0, keepdims=True),
            jnp.sum(lat_enter[...] * state, axis=0, keepdims=True),
        ]

    lon_corner[0] = jnp.concatenate(
        corners(lon_state[0]) + corners(lon_state[1]) + [jnp.zeros((4, MODES), F32)], axis=0
    )
    t1 = [
        push(lon_corner.at[0], lon_corner.at[o], t1_send.at[o], t1_recv.at[o], {"lon": lon_peer(o)})
        for o in LON_PEERS
    ]
    l1 = push(lon_state.at[1 - core], pair_buf, pair_send.at[0], pair_recv.at[0], {"lon": partner})

    early_states(innov_rows, early_lat, lat_state)
    b1 = []
    for m in LAT_PEERS:
        top = m.bit_length() - 1
        b1.append(
            push(
                lat_state.at[q_bits[top]], lat_buf.at[m], b1_send.at[m], b1_recv.at[m],
                {"lat": lat_peer(m)},
            )
        )
    lat_buf[0] = lat_state[0]

    value[...] = seg_ref[...] * innov_rows[...]
    scatter(cell_ref, value, acc, 0, 1)

    l1.wait_recv()
    chip_state = pair_buf[...] + lon_grow[pl.ds(partner, 1), :] * lon_state[core]
    chip_buf[0] = chip_state
    sign = 1 - 2 * core
    l2 = [
        push(
            chip_buf.at[0], chip_buf.at[o], l2_send.at[o], l2_recv.at[o],
            {"lon": 2 * ((z + sign * o + 8) % 8) + core},
        )
        for o in CHIP_PEERS
    ]
    scatter(cell_ref, value, acc, 1, 3)

    for copy in t1:
        copy.wait_recv()
    ahead = lon_corner[0]
    behind = lon_corner[0]
    for o in reversed(range(1, TILES)):
        ahead = lon_grow[pl.ds((p + TILES - o) % TILES, 1), :] * ahead + lon_corner[o]
        behind = lon_grow[pl.ds((p + o) % TILES, 1), :] * behind + lon_corner[TILES - o]
    sub = lax.broadcasted_iota(jnp.int32, (8, MODES), 0)
    lat_corner[0] = jnp.where(sub < 2, ahead, behind) * loop_scale
    t2 = [
        push(lat_corner.at[0], lat_corner.at[m], t2_send.at[m], t2_recv.at[m], {"lat": lat_peer(m)})
        for m in LAT_PEERS
    ]

    scatter(cell_ref, value, acc, 3, 4)

    modes_high, modes_low = split(modes_ref[...])
    both = jnp.concatenate([modes_high, modes_low], axis=1)
    to_modes = jnp.concatenate([both, both], axis=0)

    for chunk in range(ROWS // 256):
        own = slice(chunk * 256, (chunk + 1) * 256)
        forcing = acc[own, 0:128] + acc[own, 128:256]
        parts = jnp.concatenate(split(forcing), axis=1)
        result = jnp.dot(parts, to_modes, preferred_element_type=F32)
        field[own, :] = result[:, 0:128] + result[:, 128:256]

    def lon_rows(cell):
        return pl.ds(cell * CELLS, CELLS)

    state = jnp.zeros((CELLS, MODES), F32)
    for cell in range(CELLS):
        own = slice(cell, cell + 1)
        state = lon_decay[own] * state + lon_var[own] * field[lon_rows(cell), :]
        smooth[lon_rows(cell), :] = state
    back = jnp.zeros((CELLS, MODES), F32)
    for cell in reversed(range(CELLS)):
        own = slice(cell, cell + 1)
        smooth[lon_rows(cell), :] = smooth[lon_rows(cell), :] + lon_var[own] * back
        back = lon_decay[own] * (back + field[lon_rows(cell), :])

    state = jnp.zeros((CELLS, MODES), F32)
    for cell in range(CELLS):
        own = slice(cell, cell + 1)
        rows = pl.ds(cell, CELLS, stride=CELLS)
        state = lat_decay[own] * state + lat_var[own] * smooth[rows, :]
        field[rows, :] = state
    back = jnp.zeros((CELLS, MODES), F32)
    for cell in reversed(range(CELLS)):
        own = slice(cell, cell + 1)
        rows = pl.ds(cell, CELLS, stride=CELLS)
        field[rows, :] = field[rows, :] + lat_var[own] * back
        back = lat_decay[own] * (back + smooth[rows, :])

    for copy in l2:
        copy.wait_recv()
    carry = chip_buf[0]
    for o in reversed(range(1, 8)):
        carry = chip_grow[pl.ds((z - sign * o + 8) % 8, 1), :] * carry + chip_buf[o]
    carry = carry * loop_scale
    lon_carry[core] = carry
    pair_buf[...] = lon_grow[pl.ds(p, 1), :] * carry + lon_state[core]
    l3 = push(pair_buf, lon_carry.at[core], pair_send.at[1], pair_recv.at[1], {"lon": partner})

    l3.wait_recv()
    row_filter(lat_decay, lat_var, lon_carry, lon_total)

    for copy in b1:
        copy.wait_recv()
    ahead = jnp.zeros((CELLS, MODES), F32)
    behind = jnp.zeros((CELLS, MODES), F32)
    for tile in range(TILES - 1):
        got = lat_buf[lat_slot(tile)]
        ahead = jnp.where(tile < q, lat_grow[tile : tile + 1, :] * ahead + got, ahead)
    for tile in reversed(range(1, TILES)):
        got = lat_buf[lat_slot(tile)]
        behind = jnp.where(tile > q, lat_grow[tile : tile + 1, :] * behind + got, behind)

    lat_carry[0] = ahead
    lat_carry[1] = behind
    row_filter(lon_decay, lon_var, lat_carry, lat_total)

    for copy in t2:
        copy.wait_recv()
    corner_ahead = jnp.zeros((8, MODES), F32)
    corner_behind = jnp.zeros((8, MODES), F32)
    for tile in range(TILES - 1):
        got = lat_corner[lat_slot(tile)]
        corner_ahead = jnp.where(
            tile < q, lat_grow[tile : tile + 1, :] * corner_ahead + got, corner_ahead
        )
    for tile in reversed(range(1, TILES)):
        got = lat_corner[lat_slot(tile)]
        corner_behind = jnp.where(
            tile > q, lat_grow[tile : tile + 1, :] * corner_behind + got, corner_behind
        )
    lat_total[0] += lon_enter[...] * corner_ahead[0:1] + lon_leave[...] * corner_ahead[2:3]
    lat_total[1] += lon_enter[...] * corner_behind[1:2] + lon_leave[...] * corner_behind[3:4]

    both = jnp.concatenate([modes_high, modes_low], axis=0)
    to_levels = jnp.concatenate([both, both], axis=1)
    per = 8
    for chunk in range(CELLS // per):
        pieces = []
        for cell in range(chunk * per, (chunk + 1) * per):
            own = slice(cell, cell + 1)
            pieces.append(
                field[lon_rows(cell), :]
                + lon_enter[own, :] * lon_total[0]
                + lon_leave[own, :] * lon_total[1]
                + lat_enter[...] * lat_total[0, own, :]
                + lat_leave[...] * lat_total[1, own, :]
            )
        whole = jnp.concatenate(split(jnp.concatenate(pieces, axis=0)), axis=1)
        result = lax.dot_general(
            whole, to_levels, (((1,), (1,)), ((), ())), preferred_element_type=F32
        )
        own = slice(chunk * per * CELLS, (chunk + 1) * per * CELLS)
        out_ref[own, :] = result[:, 0:MODES] + result[:, MODES:]

    for copy in sent:
        copy.wait_send()


def on_device(innovation, ray_id, cell_index, seg_length, vertical_modes, lon_decay, lat_decay):
    vmem = pl.BlockSpec(memory_space=pltpu.VMEM)
    tile = lambda *shape: pltpu.VMEM(shape, F32)
    sems = lambda count: pltpu.SemaphoreType.DMA((count,))
    inputs = (
        innovation.reshape(1, 64),
        ray_id.reshape(1, BLOCKS),
        cell_index.reshape(BLOCKS, SAMP),
        seg_length.reshape(BLOCKS, SAMP),
        vertical_modes,
        lon_decay,
        lat_decay,
    )
    result = pl.pallas_call(
        kernel,
        out_shape=jax.ShapeDtypeStruct((ROWS, MODES), F32),
        in_specs=[pl.BlockSpec(memory_space=pltpu.HBM)] * 7,
        out_specs=vmem,
        scratch_shapes=[
            tile(1, 64),
            pltpu.VMEM((1, BLOCKS), jnp.int32),
            pltpu.VMEM((BLOCKS, SAMP), jnp.int32),
            tile(BLOCKS, SAMP),
            tile(MODES, MODES),
            tile(MODES, TILES * CELLS),
            tile(MODES, TILES * CELLS),
            pltpu.SemaphoreType.DMA((7,)),
            tile(ROWS, 256),
            tile(ROWS, MODES),
            tile(BLOCKS, SAMP),
            tile(8, 128),
            tile(TILES, 8, 128),
            tile(TILES, 8, 128),
            tile(TILES * CELLS, MODES),
            tile(TILES * CELLS, MODES),
            tile(TILES, MODES),
            tile(TILES, MODES),
            tile(TILES // 2, MODES),
        ]
        + [tile(CELLS, MODES)] * 8
        + [
            tile(2, CELLS, MODES),
            tile(CELLS, MODES),
            tile(8, CELLS, MODES),
            tile(2, CELLS, MODES),
            tile(2, CELLS, MODES),
            tile(TILES, CELLS, MODES),
            tile(TILES, 8, MODES),
            tile(TILES, 8, MODES),
            tile(ROWS, MODES),
            tile(BLOCKS, CELLS, 2 * MODES),
            tile(BLOCKS, CELLS, 2 * MODES),
            tile(BLOCKS, 128),
            tile(2, CELLS, MODES),
            tile(2, CELLS, MODES),
            tile(2, CELLS, MODES),
        ]
        + [sems(TILES)] * 10
        + [sems(8)] * 2
        + [sems(2)] * 2,
        compiler_params=pltpu.CompilerParams(
            collective_id=0, has_side_effects=True, vmem_limit_bytes=40 * 2**20
        ),
        name="covariance",
    )(*(pltpu.with_memory_space_constraint(given, pltpu.HBM) for given in inputs))
    return result.reshape(CELLS, CELLS, MODES)


def solution(mesh):
    placed = (
        P(("lon", "lat")),
        P("lon", "lat", None),
        P("lon", "lat", None, None),
        P("lon", "lat", None, None),
        P(),
        P(),
        P(),
    )
    return jax.shard_map(
        on_device, mesh=mesh, in_specs=placed, out_specs=P("lon", "lat", None), check_vma=False
    )
```

```python
import functools

import jax
import jax.numpy as jnp
from jax import lax
from jax.experimental import pallas as pl
from jax.experimental.pallas import tpu as pltpu
from jax.sharding import PartitionSpec as P

MESH = pl.DeviceIdType.MESH
BF = jnp.bfloat16
F32 = jnp.float32
CELLS = 32
TILES = 16
MODES = 128
ROWS = CELLS * CELLS
BLOCKS = 64
SAMP = 128
LAT_PEERS = (10, 2, 8, 9, 11, 6, 14, 5, 7, 13, 15, 1, 3, 4, 12)
LON_PEERS = (8, 9, 7, 6, 10, 5, 11, 4, 12, 3, 13, 2, 14, 1, 15)
CHIP_PEERS = (4, 3, 5, 2, 6, 1, 7)


def split(value):
    high = value.astype(BF)
    return high, (value - high.astype(F32)).astype(BF)


def hot(index, count):
    place = lax.broadcasted_iota(jnp.int32, (count, index.shape[1]), 0)
    return (place == index).astype(F32).astype(BF)


def lon_of(cell):
    return lax.shift_right_logical(cell, 12)


def lat_of(cell):
    return jnp.bitwise_and(lax.shift_right_logical(cell, 7), CELLS - 1)


def cell_rows(cell_ref, block):
    cell = cell_ref[pl.ds(block, 1), :]
    lat_hot = hot(lat_of(cell), CELLS)
    lon_hot = hot(lon_of(cell), CELLS).astype(F32)
    return jnp.concatenate(
        [
            lat_hot * jnp.broadcast_to(lon_hot[row : row + 1], (CELLS, SAMP)).astype(BF)
            for row in range(CELLS)
        ],
        axis=0,
    )


def valued_levels(cell_ref, value_ref, block):
    level = jnp.bitwise_and(cell_ref[pl.ds(block, 1), :], MODES - 1)
    hit = lax.broadcasted_iota(jnp.int32, (MODES, SAMP), 0) == level
    value = value_ref[pl.ds(block, 1), :]
    high = value.astype(BF).astype(F32)
    low = value - high
    return jnp.concatenate(
        [jnp.where(hit, high, 0.0).astype(BF), jnp.where(hit, low, 0.0).astype(BF)], axis=0
    )


def scatter(cell_ref, value_ref, acc, start, stop, step=16):
    if start == 0:
        acc[...] = jnp.zeros_like(acc)

    def body(chunk, _):
        total = None
        for inner in range(0, step, 2):
            block = chunk * step + inner
            levels = jnp.concatenate(
                [valued_levels(cell_ref, value_ref, block + k) for k in range(2)], axis=1
            )
            cells = jnp.concatenate([cell_rows(cell_ref, block + k) for k in range(2)], axis=1)
            part = lax.dot_general(
                cells, levels, (((1,), (1,)), ((), ())), preferred_element_type=F32
            )
            total = part if total is None else total + part
        acc[...] += total
        return 0

    lax.fori_loop(start, stop, body, 0)


def early_sums(cell_ref, seg_ref, tables, early_lon, early_lat, start, stop, step=16):
    modes_table, lon_weights, lat_weights = tables

    def body(part, _):
        first = part * step

        def row(ref):
            return jnp.concatenate([ref[pl.ds(first + k, 1), :] for k in range(step)], axis=1)

        def twice(value, axis):
            return jnp.concatenate([value, value], axis=axis)

        cell = row(cell_ref)
        level_hot = twice(hot(jnp.bitwise_and(cell, MODES - 1), MODES), 0)
        lon_hot = hot(lon_of(cell), CELLS)
        lat_hot = hot(lat_of(cell), CELLS)
        mode = jnp.dot(modes_table, level_hot, preferred_element_type=F32) * row(seg_ref)

        def sums(weights, summed, kept, early):
            weight = jnp.dot(weights, twice(summed, 0), preferred_element_type=F32)
            high, low = split(
                jnp.concatenate([weight[:MODES] * mode, weight[MODES:] * mode], axis=0)
            )
            for inner in range(step):
                own = slice(inner * SAMP, (inner + 1) * SAMP)
                early[first + inner] = lax.dot_general(
                    twice(kept[:, own], 1),
                    jnp.concatenate([high[:, own], low[:, own]], axis=1),
                    (((1,), (1,)), ((), ())),
                    preferred_element_type=F32,
                )

        sums(lon_weights, lon_hot, lat_hot, early_lon)
        sums(lat_weights, lat_hot, lon_hot, early_lat)
        return 0

    lax.fori_loop(start, stop, body, 0)


def early_states(innov_rows, early, states, step=8):
    def body(part, total):
        for inner in range(step):
            block = part * step + inner
            innov = jnp.broadcast_to(innov_rows[pl.ds(block, 1), :], (CELLS, MODES))
            total = tuple(
                total[way] + innov * early[block, :, way * MODES : (way + 1) * MODES]
                for way in range(2)
            )
        return total

    zero = jnp.zeros((CELLS, MODES), F32)
    states[0], states[1] = lax.fori_loop(0, BLOCKS // step, body, (zero, zero))


def row_filter(decay, var, given, result):
    for way in range(2):
        state = jnp.zeros((1, MODES), F32)
        back = jnp.zeros((1, MODES), F32)
        for cell in range(CELLS):
            own = slice(cell, cell + 1)
            state = decay[own] * state + var[own] * given[way, own, :]
            result[way, own, :] = state
        for cell in reversed(range(CELLS)):
            own = slice(cell, cell + 1)
            result[way, own, :] = result[way, own, :] + var[own] * back
            back = decay[own] * (back + given[way, own, :])


def tile_sums(tables, step=4):
    def body(part, carried):
        for inner in range(step):
            fresh = []
            for table, (grow, var, gap) in zip(tables, carried):
                decay = table[pl.ds(part * step + inner, TILES, stride=CELLS), :]
                less = 1.0 - decay
                fresh.append(
                    (
                        grow * decay,
                        decay * decay * var + less * jnp.sqrt(less),
                        gap + grow * less,
                    )
                )
            carried = tuple(fresh)
        return carried

    zero = jnp.zeros((TILES, MODES), F32)
    return lax.fori_loop(0, CELLS // step, body, ((zero + 1.0, zero, zero),) * len(tables))


def own_tables(table, first, var, decay_ref, var_ref, enter_ref, leave_ref):
    decay_ref[...] = table[pl.ds(pl.multiple_of(first, CELLS), CELLS), :]
    grow = jnp.ones((1, MODES), F32)
    for cell in range(CELLS):
        decay = decay_ref[cell : cell + 1, :]
        less = 1.0 - decay
        var = decay * decay * var + less * jnp.sqrt(less)
        grow = grow * decay
        var_ref[cell : cell + 1, :] = var
        enter_ref[cell : cell + 1, :] = grow
    grow = jnp.ones((1, MODES), F32)
    for cell in reversed(range(CELLS)):
        leave_ref[cell : cell + 1, :] = grow * var_ref[cell : cell + 1, :]
        grow = grow * decay_ref[cell : cell + 1, :]


def kernel(
    innov_hbm, ray_hbm, cell_hbm, seg_hbm, modes_hbm, lon_hbm, lat_hbm, out_ref,
    innov_ref, ray_ref, cell_ref, seg_ref, modes_ref, lon_ref, lat_ref, in_sems,
    acc, field, value, innov_row, all_innov, g1_buf,
    lon_table, lat_table, lon_grow, lat_grow, chip_grow,
    lon_decay, lon_var, lon_enter, lon_leave, lat_decay, lat_var, lat_enter, lat_leave,
    lon_state, pair_buf, chip_buf, lon_carry, lat_state, lat_buf, lon_corner, lat_corner,
    smooth, early_lon, early_lat, innov_rows, lon_total, lat_total, lat_carry,
    g1_send, g1_recv, g2_send, g2_recv, t1_send, t1_recv, t2_send, t2_recv,
    b1_send, b1_recv, l2_send, l2_recv, pair_send, pair_recv,
):
    loads = [
        pltpu.make_async_copy(src, dst, in_sems.at[k])
        for k, (src, dst) in enumerate(
            (
                (innov_hbm, innov_ref),
                (lon_hbm, lon_ref),
                (lat_hbm, lat_ref),
                (cell_hbm, cell_ref),
                (ray_hbm, ray_ref),
                (seg_hbm, seg_ref),
                (modes_hbm, modes_ref),
            )
        )
    ]
    for load in loads:
        load.start()
    innov_in, lon_in, lat_in, *late_in = loads
    p, q = lax.axis_index("lon"), lax.axis_index("lat")
    z, core = p // 2, p % 2
    q_bits = [(q // 2**k) % 2 for k in range(4)]
    partner = p + 1 - 2 * core

    def lat_peer(mask):
        peer = q
        for k in range(4):
            if (mask >> k) & 1:
                peer = peer + (1 - 2 * q_bits[k]) * 2**k
        return peer

    def lat_slot(tile):
        slot = 0
        for k in range(4):
            bit = 1 - q_bits[k] if (tile >> k) & 1 else q_bits[k]
            slot = slot + bit * 2**k
        return slot

    def lon_peer(offset):
        return (p + offset) % TILES

    barrier = pltpu.get_barrier_semaphore()
    for offset in LON_PEERS:
        pl.semaphore_signal(
            barrier, inc=1, device_id={"lon": lon_peer(offset)}, device_id_type=MESH
        )
    for mask in LAT_PEERS:
        pl.semaphore_signal(
            barrier, inc=1, device_id={"lat": lat_peer(mask)}, device_id_type=MESH
        )

    sent = []

    def push(src, dst, send_sem, recv_sem, device):
        copy = pltpu.make_async_remote_copy(
            src_ref=src, dst_ref=dst, send_sem=send_sem, recv_sem=recv_sem,
            device_id=device, device_id_type=MESH,
        )
        copy.start()
        sent.append(copy)
        return copy

    innov_row[...] = jnp.zeros_like(innov_row)
    innov_in.wait()
    innov_row[0:1, 0:64] = innov_ref[...]
    row = jnp.broadcast_to(innov_row[0:1, :], (8, 128))
    both = row + pltpu.roll(row, 64, 1)
    sub = lax.broadcasted_iota(jnp.int32, (8, 128), 0)
    lane = lax.broadcasted_iota(jnp.int32, (8, 128), 1)
    mine = (sub == q // 2) & (lane // 64 == q % 2)
    g1_buf[0] = jnp.where(mine, both, 0.0)

    lon_in.wait()
    lat_in.wait()
    for part in range(4):
        span = slice(part * 128, (part + 1) * 128)
        lon_table[span, :] = lon_ref[:, span].T
        lat_table[span, :] = lat_ref[:, span].T
    (grow, var, gap), lat_sums = tile_sums((lon_table, lat_table))
    lon_grow[...] = grow
    loop, loop_gap, loop_var = grow[0:1], gap[0:1], var[0:1]
    for tile in range(1, TILES):
        own = slice(tile, tile + 1)
        loop_var = grow[own] * grow[own] * loop_var + var[own]
        loop_gap = loop_gap + loop * gap[own]
        loop = loop * grow[own]
    enter_var = loop_var / (loop_gap * (1.0 + loop))
    for tile in range(TILES - 1):
        own = slice(tile, tile + 1)
        enter_var = jnp.where(
            tile < p, grow[own] * grow[own] * enter_var + var[own], enter_var
        )
    own_tables(lon_table, p * CELLS, enter_var, lon_decay, lon_var, lon_enter, lon_leave)
    loop_scale = 1.0 / loop_gap
    for chip in range(TILES // 2):
        chip_grow[chip : chip + 1, :] = grow[2 * chip : 2 * chip + 1] * grow[2 * chip + 1 : 2 * chip + 2]

    grow, var, _ = lat_sums
    lat_grow[...] = grow
    enter_var = jnp.zeros((1, MODES), F32)
    for tile in range(TILES - 1):
        own = slice(tile, tile + 1)
        enter_var = jnp.where(
            tile < q, grow[own] * grow[own] * enter_var + var[own], enter_var
        )
    own_tables(lat_table, q * CELLS, enter_var, lat_decay, lat_var, lat_enter, lat_leave)

    for load in late_in:
        load.wait()
    modes_high, modes_low = split(modes_ref[...].T)

    def weight_table(leave, enter):
        return jnp.concatenate(
            split(jnp.concatenate([leave[...].T, enter[...].T], axis=0)), axis=1
        )

    early_tables = (
        jnp.concatenate([modes_high, modes_low], axis=1),
        weight_table(lon_leave, lon_enter),
        weight_table(lat_leave, lat_enter),
    )
    pl.semaphore_wait(barrier, 2 * (TILES - 1))
    g1 = [
        push(g1_buf.at[0], g1_buf.at[m], g1_send.at[m], g1_recv.at[m], {"lat": lat_peer(m)})
        for m in LAT_PEERS
    ]

    early_sums(cell_ref, seg_ref, early_tables, early_lon, early_lat, 0, 2)

    for copy in g1:
        copy.wait_recv()
    total = g1_buf[0]
    for slot in range(1, TILES):
        total = total + g1_buf[slot]
    all_innov[p] = total
    g2 = [
        push(all_innov.at[p], all_innov.at[p], g2_send.at[o], g2_recv.at[o], {"lon": lon_peer(o)})
        for o in LON_PEERS
    ]

    early_sums(cell_ref, seg_ref, early_tables, early_lon, early_lat, 2, 4)
    ray = jnp.broadcast_to(ray_ref[...].astype(F32), (BLOCKS, BLOCKS))
    diagonal = lax.broadcasted_iota(jnp.int32, (BLOCKS, BLOCKS), 0) == lax.broadcasted_iota(
        jnp.int32, (BLOCKS, BLOCKS), 1
    )
    ray = jnp.sum(jnp.where(diagonal, ray, 0.0), axis=1, keepdims=True).astype(jnp.int32)
    ray = jnp.broadcast_to(ray, (BLOCKS, 128))
    place = lax.broadcasted_iota(jnp.int32, (BLOCKS, 128), 1)
    row_hot = (place == ray // 128).astype(F32).astype(BF)
    lane_hot = place == ray % 128

    for copy in g2:
        copy.wait_recv()
    table = all_innov[...].reshape(128, 128)
    picked = jnp.zeros((BLOCKS, 128), F32)
    for _ in range(3):
        high = table.astype(BF)
        picked = picked + jnp.dot(row_hot, high, preferred_element_type=F32)
        table = table - high.astype(F32)
    picked = jnp.sum(jnp.where(lane_hot, picked, 0.0), axis=1, keepdims=True)
    innov_rows[...] = jnp.broadcast_to(picked, (BLOCKS, 128))
    early_states(innov_rows, early_lon, lon_state)

    def corners(state):
        return [
            jnp.sum(lat_leave[...] * state, axis=0, keepdims=True),
            jnp.sum(lat_enter[...] * state, axis=0, keepdims=True),
        ]

    lon_corner[0] = jnp.concatenate(
        corners(lon_state[0]) + corners(lon_state[1]) + [jnp.zeros((4, MODES), F32)], axis=0
    )
    t1 = [
        push(lon_corner.at[0], lon_corner.at[o], t1_send.at[o], t1_recv.at[o], {"lon": lon_peer(o)})
        for o in LON_PEERS
    ]
    l1 = push(lon_state.at[1 - core], pair_buf, pair_send.at[0], pair_recv.at[0], {"lon": partner})

    early_states(innov_rows, early_lat, lat_state)
    b1 = []
    for m in LAT_PEERS:
        top = m.bit_length() - 1
        b1.append(
            push(
                lat_state.at[q_bits[top]], lat_buf.at[m], b1_send.at[m], b1_recv.at[m],
                {"lat": lat_peer(m)},
            )
        )
    lat_buf[0] = lat_state[0]

    value[...] = seg_ref[...] * innov_rows[...]
    scatter(cell_ref, value, acc, 0, 1)

    l1.wait_recv()
    chip_state = pair_buf[...] + lon_grow[pl.ds(partner, 1), :] * lon_state[core]
    chip_buf[0] = chip_state
    sign = 1 - 2 * core
    l2 = [
        push(
            chip_buf.at[0], chip_buf.at[o], l2_send.at[o], l2_recv.at[o],
            {"lon": 2 * ((z + sign * o + 8) % 8) + core},
        )
        for o in CHIP_PEERS
    ]
    scatter(cell_ref, value, acc, 1, 3)

    for copy in t1:
        copy.wait_recv()
    ahead = lon_corner[0]
    behind = lon_corner[0]
    for o in reversed(range(1, TILES)):
        ahead = lon_grow[pl.ds((p + TILES - o) % TILES, 1), :] * ahead + lon_corner[o]
        behind = lon_grow[pl.ds((p + o) % TILES, 1), :] * behind + lon_corner[TILES - o]
    sub = lax.broadcasted_iota(jnp.int32, (8, MODES), 0)
    lat_corner[0] = jnp.where(sub < 2, ahead, behind) * loop_scale
    t2 = [
        push(lat_corner.at[0], lat_corner.at[m], t2_send.at[m], t2_recv.at[m], {"lat": lat_peer(m)})
        for m in LAT_PEERS
    ]

    scatter(cell_ref, value, acc, 3, 4)

    modes_high, modes_low = split(modes_ref[...])
    both = jnp.concatenate([modes_high, modes_low], axis=1)
    to_modes = jnp.concatenate([both, both], axis=0)

    for chunk in range(ROWS // 256):
        own = slice(chunk * 256, (chunk + 1) * 256)
        forcing = acc[own, 0:128] + acc[own, 128:256]
        parts = jnp.concatenate(split(forcing), axis=1)
        result = jnp.dot(parts, to_modes, preferred_element_type=F32)
        field[own, :] = result[:, 0:128] + result[:, 128:256]

    def lon_rows(cell):
        return pl.ds(cell * CELLS, CELLS)

    state = jnp.zeros((CELLS, MODES), F32)
    for cell in range(CELLS):
        own = slice(cell, cell + 1)
        state = lon_decay[own] * state + lon_var[own] * field[lon_rows(cell), :]
        smooth[lon_rows(cell), :] = state
    back = jnp.zeros((CELLS, MODES), F32)
    for cell in reversed(range(CELLS)):
        own = slice(cell, cell + 1)
        smooth[lon_rows(cell), :] = smooth[lon_rows(cell), :] + lon_var[own] * back
        back = lon_decay[own] * (back + field[lon_rows(cell), :])

    state = jnp.zeros((CELLS, MODES), F32)
    for cell in range(CELLS):
        own = slice(cell, cell + 1)
        rows = pl.ds(cell, CELLS, stride=CELLS)
        state = lat_decay[own] * state + lat_var[own] * smooth[rows, :]
        field[rows, :] = state
    back = jnp.zeros((CELLS, MODES), F32)
    for cell in reversed(range(CELLS)):
        own = slice(cell, cell + 1)
        rows = pl.ds(cell, CELLS, stride=CELLS)
        field[rows, :] = field[rows, :] + lat_var[own] * back
        back = lat_decay[own] * (back + smooth[rows, :])

    for copy in l2:
        copy.wait_recv()
    carry = chip_buf[0]
    for o in reversed(range(1, 8)):
        carry = chip_grow[pl.ds((z - sign * o + 8) % 8, 1), :] * carry + chip_buf[o]
    carry = carry * loop_scale
    lon_carry[core] = carry
    pair_buf[...] = lon_grow[pl.ds(p, 1), :] * carry + lon_state[core]
    l3 = push(pair_buf, lon_carry.at[core], pair_send.at[1], pair_recv.at[1], {"lon": partner})

    l3.wait_recv()
    row_filter(lat_decay, lat_var, lon_carry, lon_total)

    for copy in b1:
        copy.wait_recv()
    ahead = jnp.zeros((CELLS, MODES), F32)
    behind = jnp.zeros((CELLS, MODES), F32)
    for tile in range(TILES - 1):
        got = lat_buf[lat_slot(tile)]
        ahead = jnp.where(tile < q, lat_grow[tile : tile + 1, :] * ahead + got, ahead)
    for tile in reversed(range(1, TILES)):
        got = lat_buf[lat_slot(tile)]
        behind = jnp.where(tile > q, lat_grow[tile : tile + 1, :] * behind + got, behind)

    lat_carry[0] = ahead
    lat_carry[1] = behind
    row_filter(lon_decay, lon_var, lat_carry, lat_total)

    for copy in t2:
        copy.wait_recv()
    corner_ahead = jnp.zeros((8, MODES), F32)
    corner_behind = jnp.zeros((8, MODES), F32)
    for tile in range(TILES - 1):
        got = lat_corner[lat_slot(tile)]
        corner_ahead = jnp.where(
            tile < q, lat_grow[tile : tile + 1, :] * corner_ahead + got, corner_ahead
        )
    for tile in reversed(range(1, TILES)):
        got = lat_corner[lat_slot(tile)]
        corner_behind = jnp.where(
            tile > q, lat_grow[tile : tile + 1, :] * corner_behind + got, corner_behind
        )
    lat_total[0] += lon_enter[...] * corner_ahead[0:1] + lon_leave[...] * corner_ahead[2:3]
    lat_total[1] += lon_enter[...] * corner_behind[1:2] + lon_leave[...] * corner_behind[3:4]

    both = jnp.concatenate([modes_high, modes_low], axis=0)
    to_levels = jnp.concatenate([both, both], axis=1)
    per = 8
    for chunk in range(CELLS // per):
        pieces = []
        for cell in range(chunk * per, (chunk + 1) * per):
            own = slice(cell, cell + 1)
            pieces.append(
                field[lon_rows(cell), :]
                + lon_enter[own, :] * lon_total[0]
                + lon_leave[own, :] * lon_total[1]
                + lat_enter[...] * lat_total[0, own, :]
                + lat_leave[...] * lat_total[1, own, :]
            )
        whole = jnp.concatenate(split(jnp.concatenate(pieces, axis=0)), axis=1)
        result = lax.dot_general(
            whole, to_levels, (((1,), (1,)), ((), ())), preferred_element_type=F32
        )
        own = slice(chunk * per * CELLS, (chunk + 1) * per * CELLS)
        out_ref[own, :] = result[:, 0:MODES] + result[:, MODES:]

    for copy in sent:
        copy.wait_send()


def on_device(innovation, ray_id, cell_index, seg_length, vertical_modes, lon_decay, lat_decay):
    vmem = pl.BlockSpec(memory_space=pltpu.VMEM)
    tile = lambda *shape: pltpu.VMEM(shape, F32)
    sems = lambda count: pltpu.SemaphoreType.DMA((count,))
    inputs = (
        innovation.reshape(1, 64),
        ray_id.reshape(1, BLOCKS),
        cell_index.reshape(BLOCKS, SAMP),
        seg_length.reshape(BLOCKS, SAMP),
        vertical_modes,
        lon_decay,
        lat_decay,
    )
    result = pl.pallas_call(
        kernel,
        out_shape=jax.ShapeDtypeStruct((ROWS, MODES), F32),
        in_specs=[pl.BlockSpec(memory_space=pltpu.HBM)] * 7,
        out_specs=vmem,
        scratch_shapes=[
            tile(1, 64),
            pltpu.VMEM((1, BLOCKS), jnp.int32),
            pltpu.VMEM((BLOCKS, SAMP), jnp.int32),
            tile(BLOCKS, SAMP),
            tile(MODES, MODES),
            tile(MODES, TILES * CELLS),
            tile(MODES, TILES * CELLS),
            pltpu.SemaphoreType.DMA((7,)),
            tile(ROWS, 256),
            tile(ROWS, MODES),
            tile(BLOCKS, SAMP),
            tile(8, 128),
            tile(TILES, 8, 128),
            tile(TILES, 8, 128),
            tile(TILES * CELLS, MODES),
            tile(TILES * CELLS, MODES),
            tile(TILES, MODES),
            tile(TILES, MODES),
            tile(TILES // 2, MODES),
        ]
        + [tile(CELLS, MODES)] * 8
        + [
            tile(2, CELLS, MODES),
            tile(CELLS, MODES),
            tile(8, CELLS, MODES),
            tile(2, CELLS, MODES),
            tile(2, CELLS, MODES),
            tile(TILES, CELLS, MODES),
            tile(TILES, 8, MODES),
            tile(TILES, 8, MODES),
            tile(ROWS, MODES),
            tile(BLOCKS, CELLS, 2 * MODES),
            tile(BLOCKS, CELLS, 2 * MODES),
            tile(BLOCKS, 128),
            tile(2, CELLS, MODES),
            tile(2, CELLS, MODES),
            tile(2, CELLS, MODES),
        ]
        + [sems(TILES)] * 10
        + [sems(8)] * 2
        + [sems(2)] * 2,
        compiler_params=pltpu.CompilerParams(
            collective_id=0, has_side_effects=True, vmem_limit_bytes=40 * 2**20
        ),
        name="covariance",
    )(*(pltpu.with_memory_space_constraint(given, pltpu.HBM) for given in inputs))
    return result.reshape(CELLS, CELLS, MODES)


def solution(mesh):
    placed = (
        P(("lon", "lat")),
        P("lon", "lat", None),
        P("lon", "lat", None, None),
        P("lon", "lat", None, None),
        P(),
        P(),
        P(),
    )
    return jax.shard_map(
        on_device, mesh=mesh, in_specs=placed, out_specs=P("lon", "lat", None), check_vma=False
    )
```

```python
import functools

import jax
import jax.numpy as jnp
from jax import lax
from jax.experimental import pallas as pl
from jax.experimental.pallas import tpu as pltpu
from jax.sharding import PartitionSpec as P

MESH = pl.DeviceIdType.MESH
BF = jnp.bfloat16
F32 = jnp.float32
CELLS = 32
TILES = 16
MODES = 128
ROWS = CELLS * CELLS
BLOCKS = 64
SAMP = 128
LAT_PEERS = (10, 2, 8, 9, 11, 6, 14, 5, 7, 13, 15, 1, 3, 4, 12)
LON_PEERS = (8, 9, 7, 6, 10, 5, 11, 4, 12, 3, 13, 2, 14, 1, 15)
CHIP_PEERS = (4, 3, 5, 2, 6, 1, 7)
FAR_FIRST = (
    [("lat", 10), ("lon", 8), ("lon", 9), ("lon", 7)]
    + [("lat", mask) for mask in (9, 11, 6, 14)]
    + [("lon", offset) for offset in (6, 10, 5, 11)]
    + [("lat", mask) for mask in (2, 8, 5, 7, 13, 15)]
    + [("lon", offset) for offset in (4, 12, 3, 13)]
    + [("lat", mask) for mask in (1, 3, 4, 12)]
    + [("lon", offset) for offset in (2, 14, 1, 15)]
)


def split(value):
    high = value.astype(BF)
    return high, (value - high.astype(F32)).astype(BF)


def hot(index, count):
    place = lax.broadcasted_iota(jnp.int32, (count, index.shape[1]), 0)
    return (place == index).astype(F32).astype(BF)


def lon_of(cell):
    return lax.shift_right_logical(cell, 12)


def lat_of(cell):
    return jnp.bitwise_and(lax.shift_right_logical(cell, 7), CELLS - 1)


def cell_rows(cell_ref, block):
    cell = cell_ref[pl.ds(block, 1), :]
    lat_hot = hot(lat_of(cell), CELLS)
    lon_hot = hot(lon_of(cell), CELLS).astype(F32)
    return jnp.concatenate(
        [
            lat_hot * jnp.broadcast_to(lon_hot[row : row + 1], (CELLS, SAMP)).astype(BF)
            for row in range(CELLS)
        ],
        axis=0,
    )


def valued_levels(cell_ref, value_ref, block):
    level = jnp.bitwise_and(cell_ref[pl.ds(block, 1), :], MODES - 1)
    hit = lax.broadcasted_iota(jnp.int32, (MODES, SAMP), 0) == level
    value = value_ref[pl.ds(block, 1), :]
    high = value.astype(BF).astype(F32)
    low = value - high
    return jnp.concatenate(
        [jnp.where(hit, high, 0.0).astype(BF), jnp.where(hit, low, 0.0).astype(BF)], axis=0
    )


def scatter(cell_ref, value_ref, acc, start, stop, step=16):
    if start == 0:
        acc[...] = jnp.zeros_like(acc)

    def body(chunk, _):
        total = None
        for inner in range(0, step, 2):
            block = chunk * step + inner
            levels = jnp.concatenate(
                [valued_levels(cell_ref, value_ref, block + k) for k in range(2)], axis=1
            )
            cells = jnp.concatenate([cell_rows(cell_ref, block + k) for k in range(2)], axis=1)
            part = lax.dot_general(
                cells, levels, (((1,), (1,)), ((), ())), preferred_element_type=F32
            )
            total = part if total is None else total + part
        acc[...] += total
        return 0

    lax.fori_loop(start, stop, body, 0)


def early_sums(cell_ref, seg_ref, tables, early_lon, early_lat, start, stop, step=16):
    modes_table, lon_weights, lat_weights = tables

    def body(part, _):
        first = part * step

        def row(ref):
            return jnp.concatenate([ref[pl.ds(first + k, 1), :] for k in range(step)], axis=1)

        def twice(value, axis):
            return jnp.concatenate([value, value], axis=axis)

        cell = row(cell_ref)
        level_hot = twice(hot(jnp.bitwise_and(cell, MODES - 1), MODES), 0)
        lon_hot = hot(lon_of(cell), CELLS)
        lat_hot = hot(lat_of(cell), CELLS)
        mode = jnp.dot(modes_table, level_hot, preferred_element_type=F32) * row(seg_ref)

        def sums(weights, summed, kept, early):
            weight = jnp.dot(weights, twice(summed, 0), preferred_element_type=F32)
            high, low = split(
                jnp.concatenate([weight[:MODES] * mode, weight[MODES:] * mode], axis=0)
            )
            for inner in range(step):
                own = slice(inner * SAMP, (inner + 1) * SAMP)
                early[first + inner] = lax.dot_general(
                    twice(kept[:, own], 1),
                    jnp.concatenate([high[:, own], low[:, own]], axis=1),
                    (((1,), (1,)), ((), ())),
                    preferred_element_type=F32,
                )

        sums(lon_weights, lon_hot, lat_hot, early_lon)
        sums(lat_weights, lat_hot, lon_hot, early_lat)
        return 0

    lax.fori_loop(start, stop, body, 0)


def early_states(innov_rows, early, states, step=8):
    def body(part, total):
        for inner in range(step):
            block = part * step + inner
            innov = jnp.broadcast_to(innov_rows[pl.ds(block, 1), :], (CELLS, MODES))
            total = tuple(
                total[way] + innov * early[block, :, way * MODES : (way + 1) * MODES]
                for way in range(2)
            )
        return total

    zero = jnp.zeros((CELLS, MODES), F32)
    states[0], states[1] = lax.fori_loop(0, BLOCKS // step, body, (zero, zero))


def row_filter(decay, var, given, result):
    for way in range(2):
        state = jnp.zeros((1, MODES), F32)
        back = jnp.zeros((1, MODES), F32)
        for cell in range(CELLS):
            own = slice(cell, cell + 1)
            state = decay[own] * state + var[own] * given[way, own, :]
            result[way, own, :] = state
        for cell in reversed(range(CELLS)):
            own = slice(cell, cell + 1)
            result[way, own, :] = result[way, own, :] + var[own] * back
            back = decay[own] * (back + given[way, own, :])


def tile_sums(tables, step=8):
    def body(part, carried):
        for inner in range(step):
            fresh = []
            for table, (grow, var, gap) in zip(tables, carried):
                decay = table[pl.ds(part * step + inner, TILES, stride=CELLS), :]
                less = 1.0 - decay
                fresh.append(
                    (
                        grow * decay,
                        decay * decay * var + less * jnp.sqrt(less),
                        gap + grow * less,
                    )
                )
            carried = tuple(fresh)
        return carried

    zero = jnp.zeros((TILES, MODES), F32)
    return lax.fori_loop(0, CELLS // step, body, ((zero + 1.0, zero, zero),) * len(tables))


def own_tables(table, first, var, decay_ref, var_ref, enter_ref, leave_ref):
    decay_ref[...] = table[pl.ds(pl.multiple_of(first, CELLS), CELLS), :]
    grow = jnp.ones((1, MODES), F32)
    for cell in range(CELLS):
        decay = decay_ref[cell : cell + 1, :]
        less = 1.0 - decay
        var = decay * decay * var + less * jnp.sqrt(less)
        grow = grow * decay
        var_ref[cell : cell + 1, :] = var
        enter_ref[cell : cell + 1, :] = grow
    grow = jnp.ones((1, MODES), F32)
    for cell in reversed(range(CELLS)):
        leave_ref[cell : cell + 1, :] = grow * var_ref[cell : cell + 1, :]
        grow = grow * decay_ref[cell : cell + 1, :]


def kernel(
    innov_hbm, ray_hbm, cell_hbm, seg_hbm, modes_hbm, lon_hbm, lat_hbm, out_ref,
    innov_ref, ray_ref, cell_ref, seg_ref, modes_ref, lon_ref, lat_ref, in_sems,
    acc, field, value, innov_row, all_innov, g1_buf,
    lon_table, lat_table, lon_grow, lat_grow, chip_grow,
    lon_decay, lon_var, lon_enter, lon_leave, lat_decay, lat_var, lat_enter, lat_leave,
    lon_state, pair_buf, chip_buf, lon_carry, lat_state, lat_buf, lon_corner, lat_corner,
    smooth, early_lon, early_lat, innov_rows, lon_total, lat_total, lat_carry,
    g1_send, g1_recv, g2_send, g2_recv, t1_send, t1_recv, t2_send, t2_recv,
    b1_send, b1_recv, l2_send, l2_recv, pair_send, pair_recv,
):
    loads = [
        pltpu.make_async_copy(src, dst, in_sems.at[k])
        for k, (src, dst) in enumerate(
            (
                (innov_hbm, innov_ref),
                (lon_hbm, lon_ref),
                (lat_hbm, lat_ref),
                (cell_hbm, cell_ref),
                (ray_hbm, ray_ref),
                (seg_hbm, seg_ref),
                (modes_hbm, modes_ref),
            )
        )
    ]
    innov_in, lon_in, lat_in, *late_in = loads
    p, q = lax.axis_index("lon"), lax.axis_index("lat")
    z, core = p // 2, p % 2
    q_bits = [(q // 2**k) % 2 for k in range(4)]
    partner = p + 1 - 2 * core

    def lat_peer(mask):
        peer = q
        for k in range(4):
            if (mask >> k) & 1:
                peer = peer + (1 - 2 * q_bits[k]) * 2**k
        return peer

    def lat_slot(tile):
        slot = 0
        for k in range(4):
            bit = 1 - q_bits[k] if (tile >> k) & 1 else q_bits[k]
            slot = slot + bit * 2**k
        return slot

    def lon_peer(offset):
        return (p + offset) % TILES

    barrier = pltpu.get_barrier_semaphore()

    def greet(peers):
        for axis, peer in peers:
            device = lon_peer(peer) if axis == "lon" else lat_peer(peer)
            pl.semaphore_signal(barrier, inc=1, device_id={axis: device}, device_id_type=MESH)

    greet(FAR_FIRST[:12])
    for load in loads:
        load.start()
    greet(FAR_FIRST[12:])

    sent = []

    def push(src, dst, send_sem, recv_sem, device):
        copy = pltpu.make_async_remote_copy(
            src_ref=src, dst_ref=dst, send_sem=send_sem, recv_sem=recv_sem,
            device_id=device, device_id_type=MESH,
        )
        copy.start()
        sent.append(copy)
        return copy

    innov_row[...] = jnp.zeros_like(innov_row)
    innov_in.wait()
    innov_row[0:1, 0:64] = innov_ref[...]
    row = jnp.broadcast_to(innov_row[0:1, :], (8, 128))
    both = row + pltpu.roll(row, 64, 1)
    sub = lax.broadcasted_iota(jnp.int32, (8, 128), 0)
    lane = lax.broadcasted_iota(jnp.int32, (8, 128), 1)
    mine = (sub == q // 2) & (lane // 64 == q % 2)
    g1_buf[0] = jnp.where(mine, both, 0.0)

    lon_in.wait()
    lat_in.wait()
    for part in range(4):
        span = slice(part * 128, (part + 1) * 128)
        lon_table[span, :] = lon_ref[:, span].T
        lat_table[span, :] = lat_ref[:, span].T
    (grow, var, gap), lat_sums = tile_sums((lon_table, lat_table))
    lon_grow[...] = grow
    loop, loop_gap, loop_var = grow[0:1], gap[0:1], var[0:1]
    for tile in range(1, TILES):
        own = slice(tile, tile + 1)
        loop_var = grow[own] * grow[own] * loop_var + var[own]
        loop_gap = loop_gap + loop * gap[own]
        loop = loop * grow[own]
    enter_var = loop_var / (loop_gap * (1.0 + loop))
    for tile in range(TILES - 1):
        own = slice(tile, tile + 1)
        enter_var = jnp.where(
            tile < p, grow[own] * grow[own] * enter_var + var[own], enter_var
        )
    own_tables(lon_table, p * CELLS, enter_var, lon_decay, lon_var, lon_enter, lon_leave)
    loop_scale = 1.0 / loop_gap
    for chip in range(TILES // 2):
        chip_grow[chip : chip + 1, :] = grow[2 * chip : 2 * chip + 1] * grow[2 * chip + 1 : 2 * chip + 2]

    grow, var, _ = lat_sums
    lat_grow[...] = grow
    enter_var = jnp.zeros((1, MODES), F32)
    for tile in range(TILES - 1):
        own = slice(tile, tile + 1)
        enter_var = jnp.where(
            tile < q, grow[own] * grow[own] * enter_var + var[own], enter_var
        )
    own_tables(lat_table, q * CELLS, enter_var, lat_decay, lat_var, lat_enter, lat_leave)

    for load in late_in:
        load.wait()
    modes_high, modes_low = split(modes_ref[...].T)

    def weight_table(leave, enter):
        return jnp.concatenate(
            split(jnp.concatenate([leave[...].T, enter[...].T], axis=0)), axis=1
        )

    early_tables = (
        jnp.concatenate([modes_high, modes_low], axis=1),
        weight_table(lon_leave, lon_enter),
        weight_table(lat_leave, lat_enter),
    )
    pl.semaphore_wait(barrier, 2 * (TILES - 1))
    g1 = [
        push(g1_buf.at[0], g1_buf.at[m], g1_send.at[m], g1_recv.at[m], {"lat": lat_peer(m)})
        for m in LAT_PEERS
    ]

    early_sums(cell_ref, seg_ref, early_tables, early_lon, early_lat, 0, 2)

    for copy in g1:
        copy.wait_recv()
    total = g1_buf[0]
    for slot in range(1, TILES):
        total = total + g1_buf[slot]
    all_innov[p] = total
    g2 = [
        push(all_innov.at[p], all_innov.at[p], g2_send.at[o], g2_recv.at[o], {"lon": lon_peer(o)})
        for o in LON_PEERS
    ]

    early_sums(cell_ref, seg_ref, early_tables, early_lon, early_lat, 2, 4)
    ray = jnp.broadcast_to(ray_ref[...].astype(F32), (BLOCKS, BLOCKS))
    diagonal = lax.broadcasted_iota(jnp.int32, (BLOCKS, BLOCKS), 0) == lax.broadcasted_iota(
        jnp.int32, (BLOCKS, BLOCKS), 1
    )
    ray = jnp.sum(jnp.where(diagonal, ray, 0.0), axis=1, keepdims=True).astype(jnp.int32)
    ray = jnp.broadcast_to(ray, (BLOCKS, 128))
    place = lax.broadcasted_iota(jnp.int32, (BLOCKS, 128), 1)
    row_hot = (place == ray // 128).astype(F32).astype(BF)
    lane_hot = place == ray % 128

    for copy in g2:
        copy.wait_recv()
    table = all_innov[...].reshape(128, 128)
    picked = jnp.zeros((BLOCKS, 128), F32)
    for _ in range(3):
        high = table.astype(BF)
        picked = picked + jnp.dot(row_hot, high, preferred_element_type=F32)
        table = table - high.astype(F32)
    picked = jnp.sum(jnp.where(lane_hot, picked, 0.0), axis=1, keepdims=True)
    innov_rows[...] = jnp.broadcast_to(picked, (BLOCKS, 128))
    early_states(innov_rows, early_lon, lon_state)

    def corners(state):
        return [
            jnp.sum(lat_leave[...] * state, axis=0, keepdims=True),
            jnp.sum(lat_enter[...] * state, axis=0, keepdims=True),
        ]

    lon_corner[0] = jnp.concatenate(
        corners(lon_state[0]) + corners(lon_state[1]) + [jnp.zeros((4, MODES), F32)], axis=0
    )
    t1 = [
        push(lon_corner.at[0], lon_corner.at[o], t1_send.at[o], t1_recv.at[o], {"lon": lon_peer(o)})
        for o in LON_PEERS
    ]
    l1 = push(lon_state.at[1 - core], pair_buf, pair_send.at[0], pair_recv.at[0], {"lon": partner})

    early_states(innov_rows, early_lat, lat_state)
    b1 = []
    for m in LAT_PEERS:
        top = m.bit_length() - 1
        b1.append(
            push(
                lat_state.at[q_bits[top]], lat_buf.at[m], b1_send.at[m], b1_recv.at[m],
                {"lat": lat_peer(m)},
            )
        )
    lat_buf[0] = lat_state[0]

    value[...] = seg_ref[...] * innov_rows[...]
    scatter(cell_ref, value, acc, 0, 1)

    l1.wait_recv()
    chip_state = pair_buf[...] + lon_grow[pl.ds(partner, 1), :] * lon_state[core]
    chip_buf[0] = chip_state
    sign = 1 - 2 * core
    l2 = [
        push(
            chip_buf.at[0], chip_buf.at[o], l2_send.at[o], l2_recv.at[o],
            {"lon": 2 * ((z + sign * o + 8) % 8) + core},
        )
        for o in CHIP_PEERS
    ]
    scatter(cell_ref, value, acc, 1, 3)

    for copy in t1:
        copy.wait_recv()
    ahead = lon_corner[0]
    behind = lon_corner[0]
    for o in reversed(range(1, TILES)):
        ahead = lon_grow[pl.ds((p + TILES - o) % TILES, 1), :] * ahead + lon_corner[o]
        behind = lon_grow[pl.ds((p + o) % TILES, 1), :] * behind + lon_corner[TILES - o]
    sub = lax.broadcasted_iota(jnp.int32, (8, MODES), 0)
    lat_corner[0] = jnp.where(sub < 2, ahead, behind) * loop_scale
    t2 = [
        push(lat_corner.at[0], lat_corner.at[m], t2_send.at[m], t2_recv.at[m], {"lat": lat_peer(m)})
        for m in LAT_PEERS
    ]

    scatter(cell_ref, value, acc, 3, 4)

    modes_high, modes_low = split(modes_ref[...])
    both = jnp.concatenate([modes_high, modes_low], axis=1)
    to_modes = jnp.concatenate([both, both], axis=0)

    for chunk in range(ROWS // 256):
        own = slice(chunk * 256, (chunk + 1) * 256)
        forcing = acc[own, 0:128] + acc[own, 128:256]
        parts = jnp.concatenate(split(forcing), axis=1)
        result = jnp.dot(parts, to_modes, preferred_element_type=F32)
        field[own, :] = result[:, 0:128] + result[:, 128:256]

    def lon_rows(cell):
        return pl.ds(cell * CELLS, CELLS)

    state = jnp.zeros((CELLS, MODES), F32)
    for cell in range(CELLS):
        own = slice(cell, cell + 1)
        state = lon_decay[own] * state + lon_var[own] * field[lon_rows(cell), :]
        smooth[lon_rows(cell), :] = state
    back = jnp.zeros((CELLS, MODES), F32)
    for cell in reversed(range(CELLS)):
        own = slice(cell, cell + 1)
        smooth[lon_rows(cell), :] = smooth[lon_rows(cell), :] + lon_var[own] * back
        back = lon_decay[own] * (back + field[lon_rows(cell), :])

    state = jnp.zeros((CELLS, MODES), F32)
    for cell in range(CELLS):
        own = slice(cell, cell + 1)
        rows = pl.ds(cell, CELLS, stride=CELLS)
        state = lat_decay[own] * state + lat_var[own] * smooth[rows, :]
        field[rows, :] = state
    back = jnp.zeros((CELLS, MODES), F32)
    for cell in reversed(range(CELLS)):
        own = slice(cell, cell + 1)
        rows = pl.ds(cell, CELLS, stride=CELLS)
        field[rows, :] = field[rows, :] + lat_var[own] * back
        back = lat_decay[own] * (back + smooth[rows, :])

    for copy in l2:
        copy.wait_recv()
    carry = chip_buf[0]
    for o in reversed(range(1, 8)):
        carry = chip_grow[pl.ds((z - sign * o + 8) % 8, 1), :] * carry + chip_buf[o]
    carry = carry * loop_scale
    lon_carry[core] = carry
    pair_buf[...] = lon_grow[pl.ds(p, 1), :] * carry + lon_state[core]
    l3 = push(pair_buf, lon_carry.at[core], pair_send.at[1], pair_recv.at[1], {"lon": partner})

    l3.wait_recv()
    row_filter(lat_decay, lat_var, lon_carry, lon_total)

    for copy in b1:
        copy.wait_recv()
    ahead = jnp.zeros((CELLS, MODES), F32)
    behind = jnp.zeros((CELLS, MODES), F32)
    for tile in range(TILES - 1):
        got = lat_buf[lat_slot(tile)]
        ahead = jnp.where(tile < q, lat_grow[tile : tile + 1, :] * ahead + got, ahead)
    for tile in reversed(range(1, TILES)):
        got = lat_buf[lat_slot(tile)]
        behind = jnp.where(tile > q, lat_grow[tile : tile + 1, :] * behind + got, behind)

    lat_carry[0] = ahead
    lat_carry[1] = behind
    row_filter(lon_decay, lon_var, lat_carry, lat_total)

    for copy in t2:
        copy.wait_recv()
    corner_ahead = jnp.zeros((8, MODES), F32)
    corner_behind = jnp.zeros((8, MODES), F32)
    for tile in range(TILES - 1):
        got = lat_corner[lat_slot(tile)]
        corner_ahead = jnp.where(
            tile < q, lat_grow[tile : tile + 1, :] * corner_ahead + got, corner_ahead
        )
    for tile in reversed(range(1, TILES)):
        got = lat_corner[lat_slot(tile)]
        corner_behind = jnp.where(
            tile > q, lat_grow[tile : tile + 1, :] * corner_behind + got, corner_behind
        )
    lat_total[0] += lon_enter[...] * corner_ahead[0:1] + lon_leave[...] * corner_ahead[2:3]
    lat_total[1] += lon_enter[...] * corner_behind[1:2] + lon_leave[...] * corner_behind[3:4]

    both = jnp.concatenate([modes_high, modes_low], axis=0)
    to_levels = jnp.concatenate([both, both], axis=1)
    per = 8
    for chunk in range(CELLS // per):
        pieces = []
        for cell in range(chunk * per, (chunk + 1) * per):
            own = slice(cell, cell + 1)
            pieces.append(
                field[lon_rows(cell), :]
                + lon_enter[own, :] * lon_total[0]
                + lon_leave[own, :] * lon_total[1]
                + lat_enter[...] * lat_total[0, own, :]
                + lat_leave[...] * lat_total[1, own, :]
            )
        whole = jnp.concatenate(split(jnp.concatenate(pieces, axis=0)), axis=1)
        result = lax.dot_general(
            whole, to_levels, (((1,), (1,)), ((), ())), preferred_element_type=F32
        )
        own = slice(chunk * per * CELLS, (chunk + 1) * per * CELLS)
        out_ref[own, :] = result[:, 0:MODES] + result[:, MODES:]

    for copy in sent:
        copy.wait_send()


def on_device(innovation, ray_id, cell_index, seg_length, vertical_modes, lon_decay, lat_decay):
    vmem = pl.BlockSpec(memory_space=pltpu.VMEM)
    tile = lambda *shape: pltpu.VMEM(shape, F32)
    sems = lambda count: pltpu.SemaphoreType.DMA((count,))
    inputs = (
        innovation.reshape(1, 64),
        ray_id.reshape(1, BLOCKS),
        cell_index.reshape(BLOCKS, SAMP),
        seg_length.reshape(BLOCKS, SAMP),
        vertical_modes,
        lon_decay,
        lat_decay,
    )
    result = pl.pallas_call(
        kernel,
        out_shape=jax.ShapeDtypeStruct((ROWS, MODES), F32),
        in_specs=[pl.BlockSpec(memory_space=pltpu.HBM)] * 7,
        out_specs=vmem,
        scratch_shapes=[
            tile(1, 64),
            pltpu.VMEM((1, BLOCKS), jnp.int32),
            pltpu.VMEM((BLOCKS, SAMP), jnp.int32),
            tile(BLOCKS, SAMP),
            tile(MODES, MODES),
            tile(MODES, TILES * CELLS),
            tile(MODES, TILES * CELLS),
            pltpu.SemaphoreType.DMA((7,)),
            tile(ROWS, 256),
            tile(ROWS, MODES),
            tile(BLOCKS, SAMP),
            tile(8, 128),
            tile(TILES, 8, 128),
            tile(TILES, 8, 128),
            tile(TILES * CELLS, MODES),
            tile(TILES * CELLS, MODES),
            tile(TILES, MODES),
            tile(TILES, MODES),
            tile(TILES // 2, MODES),
        ]
        + [tile(CELLS, MODES)] * 8
        + [
            tile(2, CELLS, MODES),
            tile(CELLS, MODES),
            tile(8, CELLS, MODES),
            tile(2, CELLS, MODES),
            tile(2, CELLS, MODES),
            tile(TILES, CELLS, MODES),
            tile(TILES, 8, MODES),
            tile(TILES, 8, MODES),
            tile(ROWS, MODES),
            tile(BLOCKS, CELLS, 2 * MODES),
            tile(BLOCKS, CELLS, 2 * MODES),
            tile(BLOCKS, 128),
            tile(2, CELLS, MODES),
            tile(2, CELLS, MODES),
            tile(2, CELLS, MODES),
        ]
        + [sems(TILES)] * 10
        + [sems(8)] * 2
        + [sems(2)] * 2,
        compiler_params=pltpu.CompilerParams(
            collective_id=0, has_side_effects=True, vmem_limit_bytes=40 * 2**20
        ),
        name="covariance",
    )(*(pltpu.with_memory_space_constraint(given, pltpu.HBM) for given in inputs))
    return result.reshape(CELLS, CELLS, MODES)


def solution(mesh):
    placed = (
        P(("lon", "lat")),
        P("lon", "lat", None),
        P("lon", "lat", None, None),
        P("lon", "lat", None, None),
        P(),
        P(),
        P(),
    )
    return jax.shard_map(
        on_device, mesh=mesh, in_specs=placed, out_specs=P("lon", "lat", None), check_vma=False
    )
```
